512 devices in a mesh: dp: 4 (over x), bank: 128 (over z, y, core).
Axes of the slice: x: 4, y: 4, z: 16, core: 2. Of those that a mesh axis runs over, the one named last changes fastest.
Arguments:
- frames: bfloat16 [8192, 1280], P(('dp', 'bank')), may hold values from -6 to 6
- ln_gain: float32 [1280], replicated, may hold values from 0.5 to 1.5
- w_query: bfloat16 [1280, 256], replicated, may hold values from -0.15625 to 0.15625
- bank_keys: bfloat16 [131072, 256], P('bank'), may hold values from -6 to 6
- bank_values: bfloat16 [131072, 256], P('bank'), may hold values from -6 to 6
- active: int32 [4, 256], replicated, may hold values from 0 to 1023, as said below
- w_out: bfloat16 [256, 1280], replicated, may hold values from -0.375 to 0.375
- ffn_gain: float32 [1280], replicated, may hold values from 0.5 to 1.5
- w_up: bfloat16 [1280, 2560], P(None, 'dp'), may hold values from -0.15625 to 0.15625
- w_down: bfloat16 [2560, 1280], P('dp'), may hold values from -0.125 to 0.125
Outputs:
- layer_out: bfloat16 [8192, 1280], P(('dp', 'bank'))
The draws below stay inside these ranges and needn't reach their ends.
Inputs may be any that keep to these rules, and one draw needn't show every extreme that they name: `active`: each row lists 256 phrase block ids of one stream; ids may repeat.
All inputs are finite; a program needn't handle non-finite values.
Results may differ from the reference program's by a relative error of at most 0.012.
Values may be sent and summed in bfloat16 or wider, within the bound.
A program may use at most 64 MiB of HBM per device.

```python
import jax
import jax.numpy as jnp
from jax import lax

D = 1280
FF = 2560
BIAS = 256
BLK = 128
LEN = 2048
STREAMS = 4
PHRASES = 131072
BLOCKS = 1024
NACT = 256


def draw_bank_values(key, part):
    key = jax.random.fold_in(key, 11)
    values = jax.random.truncated_normal(key, -6.0, 6.0, (PHRASES, BIAS), jnp.float32)
    return values.astype(jnp.bfloat16)


def draw_active(key, part):
    key = jax.random.fold_in(key, 7)
    stream_keys = jax.random.split(key, STREAMS)
    chosen = jax.vmap(lambda single: jax.random.permutation(single, BLOCKS)[:NACT])(stream_keys)
    chosen = chosen.astype(jnp.int32)
    chosen = chosen.at[0, 0].set(BLOCKS - 1)
    chosen = chosen.at[STREAMS - 1, NACT - 1].set(0)
    return chosen


def level_of(stream_key, dims, shards, least, largest):
    loudness = 1.0
    for axis_at, blocks in shards:
        draws = jax.random.uniform(jax.random.fold_in(jax.random.fold_in(stream_key, 6), axis_at), (blocks,), jnp.float32, least / len(shards), largest / len(shards))
        loudness = loudness * jnp.repeat(jnp.exp(draws), dims[axis_at] // blocks).reshape((-1,) + (1,) * (len(dims) - 1 - axis_at))
    return loudness


def noise(key, shape, width, bound, cuts=(), kind=jnp.bfloat16):
    loudness = level_of(key, shape, cuts, -0.22, 0.18) if cuts else 1.0
    values = jax.random.normal(key, shape, jnp.float32) * width * loudness
    return jnp.minimum(jnp.maximum(values, -bound), bound).astype(kind)


def setup_inputs(seed: int = 0) -> dict:
    splits = jax.random.split(jax.random.key(seed), 11)
    return {
        "frames": noise(splits[0], (STREAMS * LEN, D), 1.0, 6.0, ((0, 512),)),
        "ln_gain": jnp.clip(1.0 + 0.1 * jax.random.normal(splits[1], (D,), jnp.float32), 0.5, 1.5),
        "w_query": noise(splits[2], (D, BIAS), D ** -0.5, 0.15625),
        "bank_keys": noise(splits[3], (PHRASES, BIAS), 1.0, 6.0, ((0, 128),)),
        "bank_values": draw_bank_values(jax.random.fold_in(splits[10], 71), 0),
        "active": draw_active(jax.random.fold_in(splits[10], 71), 0),
        "w_out": noise(splits[6], (BIAS, D), BIAS ** -0.5, 0.375),
        "ffn_gain": jnp.clip(1.0 + 0.1 * jax.random.normal(splits[7], (D,), jnp.float32), 0.5, 1.5),
        "w_up": noise(splits[8], (D, FF), D ** -0.5, 0.15625, ((1, 4),)),
        "w_down": noise(splits[9], (FF, D), FF ** -0.5, 0.125, ((0, 4),)),
    }


softcap = 30.0

def layer_norm(values, gain_vector):
    wide = values.astype(jnp.float32)
    center = lax.optimization_barrier(jnp.mean(wide, axis=-1, keepdims=True))
    spread = lax.optimization_barrier(jnp.mean((wide - center) ** 2, axis=-1, keepdims=True))
    return (wide - center) * lax.rsqrt(spread + 1e-05) * gain_vector

def reference(frames, ln_gain, w_query, bank_keys, bank_values, active, w_out, ffn_gain, w_up, w_down):
    normed = layer_norm(frames, ln_gain).astype(jnp.bfloat16)
    queries = jnp.dot(normed, w_query, preferred_element_type=jnp.float32).astype(jnp.bfloat16)
    block_count = PHRASES // BLK
    tile_len = min(4096, PHRASES)
    tile_count = PHRASES // tile_len
    key_tiles = bank_keys.reshape(tile_count, tile_len, BIAS)
    value_tiles = bank_values.reshape(tile_count, tile_len, BIAS)
    score_scale = 1.0 / (softcap * BIAS ** 0.5)
    contexts = []
    for stream in range(STREAMS):
        stream_rows = queries[stream * LEN:(stream + 1) * LEN]
        block_flags = jnp.any(jnp.arange(block_count, dtype=jnp.int32)[:, None] == active[stream][None, :], axis=1)
        allowed = jnp.repeat(block_flags, BLK).reshape(tile_count, tile_len)

        def visit(state_pair, tile):
            key_tile, value_tile, allow_tile = tile
            raw = lax.dot_general(stream_rows, key_tile, (((1,), (1,)), ((), ())), preferred_element_type=jnp.float32)
            score = softcap * jnp.tanh(raw * score_scale)
            weight = jnp.where(allow_tile[None, :], jnp.exp(score), jnp.float32(0.0))
            numerator = state_pair[0] + jnp.dot(weight.astype(jnp.bfloat16), value_tile, preferred_element_type=jnp.float32)
            totals = state_pair[1] + lax.optimization_barrier(jnp.sum(weight, axis=1))
            return ((numerator, totals), None)
        start_pair = (jnp.zeros((LEN, BIAS), jnp.float32), jnp.zeros((LEN,), jnp.float32))
        final_pair, unused = lax.scan(visit, start_pair, (key_tiles, value_tiles, allowed))
        contexts.append(final_pair[0] / final_pair[1][:, None])
    context = jnp.concatenate(contexts, axis=0)
    context_norm = (context * lax.rsqrt(lax.optimization_barrier(jnp.mean(context * context, axis=1, keepdims=True)) + 0.0001)).astype(jnp.bfloat16)
    residual = (frames.astype(jnp.float32) + jnp.dot(context_norm, w_out, preferred_element_type=jnp.float32)).astype(jnp.bfloat16)
    ffn_in = layer_norm(residual, ffn_gain).astype(jnp.bfloat16)
    hidden = jax.nn.gelu(jnp.dot(ffn_in, w_up, preferred_element_type=jnp.float32), approximate=False).astype(jnp.bfloat16)
    return (residual.astype(jnp.float32) + jnp.dot(hidden, w_down, preferred_element_type=jnp.float32)).astype(jnp.bfloat16)
```

```python
import jax
import jax.numpy as jnp
from jax import lax
from jax.experimental import pallas as pl
from jax.experimental.pallas import tpu as pltpu
from jax.sharding import PartitionSpec as P

MESH = pl.DeviceIdType.MESH
F32 = jnp.float32
BF16 = jnp.bfloat16
CAP = 30.0
LOG2E = 1.4426950408889634
NEAR = (0, 1, -1, 2, -2, 3, -3, 4)
NZ, NY, NX = 16, 4, 4
D, FFL, BIAS = 1280, 640, 256
ROWS = 16
PH = 1024
WIDE = BIAS + 128
STEP = 256


def layer_norm(values, gain_row):
    wide = values.astype(F32)
    center = jnp.mean(wide, axis=-1, keepdims=True)
    moved = wide - center
    spread = jnp.mean(moved * moved, axis=-1, keepdims=True)
    return moved * lax.rsqrt(spread + 1e-05) * gain_row


def gelu(v):
    return 0.5 * v * (1.0 + lax.erf(v * 0.7071067811865476))


def kernel(
    frames, ln_gain, w_query, keys, values, active, w_out, ffn_gain, w_up, w_down, out,
    fr, lng, ffg, wq, kb, vb, act, wo, wu, wd,
    qown, qb, pb, po, ry, zs, rz, rs, yo, xr, rc, bias,
    ld, s_kv, r_kv, s_fr, r_fr, s_qx, r_qx, s_q, r_q, s_yf, r_yf, s_ry, r_ry, s_rz, r_rz,
    s_xa, r_xa, s_xr, r_xr, s_rc, r_rc,
):
    x = lax.axis_index("dp")
    b = lax.axis_index("bank")
    c = lax.rem(b, 2)
    y = lax.rem(b // 2, NY)
    z = b // (2 * NY)

    def dev(dx=0, dz=0, dy=0, core=None):
        cz = lax.rem(z + dz + 2 * NZ, NZ)
        cy = lax.rem(y + dy + NY, NY)
        return (lax.rem(x + dx + NX, NX), (cz * NY + cy) * 2 + (c if core is None else core))

    sibling = dev(core=1 - c)

    def send(src, dst, ssem, rsem, to):
        return pltpu.make_async_remote_copy(
            src_ref=src, dst_ref=dst, send_sem=ssem, recv_sem=rsem, device_id=to, device_id_type=MESH
        )

    def arrived(dst, rsem):
        send(dst, dst, rsem, rsem, sibling).wait_recv()

    def far(i):
        return NEAR[i] + (4 if i % 2 else -4) * c

    loads = [
        pltpu.make_async_copy(src, dst, ld.at[n])
        for n, (src, dst) in enumerate(
            (
                (frames, fr.at[pl.ds(ROWS, ROWS)]),
                (ln_gain, lng),
                (w_query, wq),
                (active, act),
                (keys, kb.at[c]),
                (values, vb.at[c]),
                (w_out, wo),
                (ffn_gain, ffg),
                (w_up, wu),
                (w_down, wd),
            )
        )
    ]
    for load in loads:
        load.start()

    barrier = pltpu.get_barrier_semaphore()

    def greet(to):
        pl.semaphore_signal(barrier, inc=1, device_id=to, device_id_type=MESH)

    @pl.when(c == 1)
    def _():
        for dz in (8, 7, -7, 6, -6, 5, -5, 4, -4):
            greet(dev(dz=dz, core=1))
        for dz in NEAR[::-1]:
            greet(dev(dz=-dz, core=0))
        for e in (2, 1, 3):
            greet(dev(dy=e))
            greet(dev(dx=e, core=0))
            greet(dev(dx=e, core=1))

    @pl.when(c == 0)
    def _():
        for dz in NEAR[::-1]:
            greet(dev(dz=dz, core=1))
        for e in (2, 1, 3):
            greet(dev(dy=e))
            greet(dev(dx=e, core=1))

    for n in range(4):
        loads[n].wait()
    normed = layer_norm(fr[ROWS:, :], lng[...]).astype(BF16)
    qown[pl.ds(ROWS, ROWS), :] = jnp.dot(normed, wq[...], preferred_element_type=F32).astype(BF16)

    first = (z * NY + y) * 16
    ids = first + lax.broadcasted_iota(jnp.int32, (16, 256), 0)
    hits = jnp.where(ids == act[pl.ds(x, 1), :], 1.0, 0.0).astype(F32)
    found = jnp.max(hits, axis=1, keepdims=True)
    bias[...] = jnp.broadcast_to(jnp.where(found > 0.5, 0.0, -512.0).astype(F32), (16, 128))

    keys_over = send(keys, kb.at[c], s_kv.at[0], r_kv.at[0], sibling)
    values_over = send(values, vb.at[c], s_kv.at[1], r_kv.at[1], sibling)
    query_over = send(qown.at[pl.ds(ROWS, ROWS)], qown.at[pl.ds(0, ROWS)], s_qx, r_qx, sibling)
    frames_over = send(frames, fr.at[pl.ds(0, ROWS)], s_fr, r_fr, sibling)
    query_out = []
    for core in (1, 0):
        for i in range(7, -1, -1):
            dz = NEAR[i] + (4 if i % 2 else -4) * core
            query_out.append(
                send(
                    qown,
                    qb.at[i // 2, 0, pl.ds((i % 2) * 2 * ROWS, 2 * ROWS)],
                    s_q.at[core * 8 + i],
                    r_q.at[i],
                    dev(dz=-dz, core=core),
                )
            )

    @pl.when(c == 0)
    def _():
        pl.semaphore_wait(barrier, 14)
        query_over.start()

    @pl.when(c == 1)
    def _():
        pl.semaphore_wait(barrier, 26)
        arrived(qown.at[pl.ds(0, ROWS)], r_qx)
        for copy in query_out:
            copy.start()

    keys_over.start()
    values_over.start()

    @pl.when(c == 0)
    def _():
        frames_over.start()

    forward = []
    for k in range(4):
        for j in range(2):
            arrived(qb.at[k, 0, pl.ds(j * 2 * ROWS, 2 * ROWS)], r_q.at[2 * k + j])
        for e in (2, 1, 3):
            copy = send(qb.at[k, 0], qb.at[k, NY - e], s_yf.at[k, e - 1], r_yf.at[k, NY - e - 1], dev(dy=e))
            copy.start()
            forward.append(copy)

    for n in range(4, 6):
        loads[n].wait()
    arrived(kb.at[1 - c], r_kv.at[0])
    arrived(vb.at[1 - c], r_kv.at[1])

    def give_back(k, e):
        return send(pb.at[k, e - 1], ry.at[k, NY - e - 1], s_ry.at[k, e - 1], r_ry.at[k, NY - e - 1], dev(dy=e))

    scale = 1.0 / (CAP * BIAS**0.5)

    def attend(k, carry):
        for e in (1, 3, 2):
            arrived(qb.at[k, e], r_yf.at[k, e - 1])
        q = qb[k].reshape(STEP, BIAS)
        num = jnp.zeros((STEP, BIAS), F32)
        tot = jnp.zeros((STEP, 128), F32)
        for p in range(2 * PH // STEP):
            h, at = (p * STEP) // PH, (p * STEP) % PH
            raw = lax.dot_general(
                q, kb[h, pl.ds(at, STEP), :], (((1,), (1,)), ((), ())), preferred_element_type=F32
            )
            off = jnp.concatenate([bias[pl.ds(2 * p, 1), :], bias[pl.ds(2 * p + 1, 1), :]], axis=1)
            weight = jnp.exp2(jnp.tanh(raw * scale) * (CAP * LOG2E) + off)
            tot = tot + (weight[:, :128] + weight[:, 128:])
            num = num + jnp.dot(weight.astype(BF16), vb[h, pl.ds(at, STEP), :], preferred_element_type=F32)
        part = 4 * ROWS
        po[k, :, :BIAS] = num[:part]
        po[k, :, BIAS:] = tot[:part]
        for e in (1, 2, 3):
            pb[k, e - 1, :, :BIAS] = num[e * part : (e + 1) * part].astype(BF16)
            pb[k, e - 1, :, BIAS:] = tot[e * part : (e + 1) * part].astype(BF16)
        for e in (2, 1, 3):
            give_back(k, e).start()
        return carry

    lax.fori_loop(0, 4, attend, 0)

    sums_out = []
    for k in range(4):
        total = po[k]
        for e in (1, 3, 2):
            arrived(ry.at[k, e - 1], r_ry.at[k, e - 1])
            total = total + ry[k, e - 1].astype(F32)
        zs[k] = total.astype(BF16)
        for j in (1, 0):
            i = 2 * k + j
            copy = send(
                zs.at[k, pl.ds(j * 2 * ROWS, 2 * ROWS)],
                rz.at[c * 8 + i],
                s_rz.at[i],
                r_rz.at[c * 8 + i],
                dev(dz=far(i), core=1),
            )
            copy.start()
            sums_out.append(copy)

    for n in range(6, 10):
        loads[n].wait()

    residual_out = [
        send(rs.at[0], rs.at[NX - e], s_xa.at[e - 1], r_xa.at[NX - e - 1], dev(dx=e)) for e in (2, 1, 3)
    ]
    residual_over = send(rs.at[0, pl.ds(0, ROWS)], rc, s_rc, r_rc, sibling)
    parts_out = [
        send(
            yo.at[e, pl.ds(core * ROWS, ROWS)],
            xr.at[(NX - e) % NX],
            s_xr.at[e * 2 + core],
            r_xr.at[(NX - e) % NX],
            dev(dx=e, core=core),
        )
        for e, core in ((2, 0), (2, 1), (1, 0), (1, 1), (3, 0), (3, 1), (0, 0))
    ]

    @pl.when(c == 1)
    def _():
        arrived(fr.at[pl.ds(0, ROWS)], r_fr)
        total = jnp.zeros((2 * ROWS, WIDE), F32)
        for n in range(16):
            arrived(rz.at[n], r_rz.at[n])
            total = total + rz[n].astype(F32)
        context = total[:, :BIAS] / jnp.sum(total[:, BIAS:], axis=1, keepdims=True)
        power = jnp.mean(context * context, axis=1, keepdims=True)
        context_norm = (context * lax.rsqrt(power + 0.0001)).astype(BF16)
        residual = fr[...].astype(F32) + jnp.dot(context_norm, wo[...], preferred_element_type=F32)
        rs[0] = residual.astype(BF16)
        for copy in residual_out:
            copy.start()
        residual_over.start()
        for e in (1, 3, 2):
            arrived(rs.at[e], r_xa.at[e - 1])
        ffn_in = layer_norm(rs[...].reshape(NX * 2 * ROWS, D), ffg[...]).astype(BF16)
        hidden = gelu(jnp.dot(ffn_in, wu[...], preferred_element_type=F32)).astype(BF16)
        part = jnp.dot(hidden, wd[...], preferred_element_type=F32).astype(BF16)
        yo[...] = part.reshape(NX, 2 * ROWS, D)
        for copy in parts_out:
            copy.start()
        done = rs[0, ROWS:, :].astype(F32) + yo[0, ROWS:, :].astype(F32)
        for e in (1, 3, 2):
            arrived(xr.at[e], r_xr.at[e])
            done = done + xr[e].astype(F32)
        out[...] = done.astype(BF16)

    @pl.when(c == 0)
    def _():
        arrived(rc, r_rc)
        done = rc[...].astype(F32)
        for e in (0, 1, 3, 2):
            arrived(xr.at[e], r_xr.at[e])
            done = done + xr[e].astype(F32)
        out[...] = done.astype(BF16)

    keys_over.wait_send()
    values_over.wait_send()
    for copy in forward + sums_out:
        copy.wait_send()
    for k in range(4):
        for e in (1, 2, 3):
            give_back(k, e).wait_send()

    @pl.when(c == 0)
    def _():
        query_over.wait_send()
        frames_over.wait_send()

    @pl.when(c == 1)
    def _():
        for copy in query_out + residual_out + parts_out:
            copy.wait_send()
        residual_over.wait_send()


def local(*args):
    dma = pltpu.SemaphoreType.DMA
    vm = pltpu.VMEM
    rows = 2 * ROWS
    return pl.pallas_call(
        kernel,
        out_shape=jax.ShapeDtypeStruct((ROWS, D), BF16),
        in_specs=[pl.BlockSpec(memory_space=pl.ANY)] * 10,
        out_specs=pl.BlockSpec(memory_space=pltpu.VMEM),
        scratch_shapes=[
            vm((rows, D), BF16),
            vm((1, D), F32),
            vm((1, D), F32),
            vm((D, BIAS), BF16),
            vm((2, PH, BIAS), BF16),
            vm((2, PH, BIAS), BF16),
            vm((4, 256), jnp.int32),
            vm((BIAS, D), BF16),
            vm((D, FFL), BF16),
            vm((FFL, D), BF16),
            vm((rows, BIAS), BF16),
            vm((4, NY, 2 * rows, BIAS), BF16),
            vm((4, 3, 2 * rows, WIDE), BF16),
            vm((4, 2 * rows, WIDE), F32),
            vm((4, 3, 2 * rows, WIDE), BF16),
            vm((4, 2 * rows, WIDE), BF16),
            vm((16, rows, WIDE), BF16),
            vm((NX, rows, D), BF16),
            vm((NX, rows, D), BF16),
            vm((NX, ROWS, D), BF16),
            vm((ROWS, D), BF16),
            vm((16, 128), F32),
            dma((10,)),
            dma((2,)), dma((2,)),
            dma, dma,
            dma, dma,
            dma((16,)), dma((8,)),
            dma((4, 3)), dma((4, 3)),
            dma((4, 3)), dma((4, 3)),
            dma((8,)), dma((16,)),
            dma((3,)), dma((3,)),
            dma((8,)), dma((4,)),
            dma, dma,
        ],
        compiler_params=pltpu.CompilerParams(
            collective_id=0, has_side_effects=True, vmem_limit_bytes=48 * 2**20
        ),
        name="layer",
    )(*args)


def solution(mesh):
    placed = (
        P(("dp", "bank"), None),
        P(None, None),
        P(),
        P("bank", None),
        P("bank", None),
        P(),
        P(),
        P(None, None),
        P(None, "dp"),
        P("dp", None),
    )
    whole = jax.shard_map(
        local, mesh=mesh, in_specs=placed, out_specs=P(("dp", "bank"), None), check_vma=False
    )

    def step(frames, ln_gain, w_query, bank_keys, bank_values, active, w_out, ffn_gain, w_up, w_down):
        return whole(
            frames, ln_gain[None], w_query, bank_keys, bank_values, active, w_out, ffn_gain[None], w_up, w_down
        )

    return step
```

```python
import jax
import jax.numpy as jnp
from jax import lax
from jax.experimental import pallas as pl
from jax.experimental.pallas import tpu as pltpu
from jax.sharding import PartitionSpec as P

MESH = pl.DeviceIdType.MESH
F32 = jnp.float32
BF16 = jnp.bfloat16
CAP = 30.0
LOG2E = 1.4426950408889634
NEAR = (0, 1, -1, 2, -2, 3, -3, 4)
NZ, NY, NX = 16, 4, 4
D, FFL, BIAS = 1280, 640, 256
ROWS = 16
PH = 1024
WIDE = BIAS + 128
STEP = 256


def layer_norm(values, gain):
    wide = values.astype(F32)
    center = jnp.mean(wide, axis=-1, keepdims=True)
    moved = wide - center
    spread = jnp.mean(moved * moved, axis=-1, keepdims=True)
    return moved * lax.rsqrt(spread + 1e-05) * gain[None, :]


def gelu(v):
    return 0.5 * v * (1.0 + lax.erf(v * 0.7071067811865476))


def kernel(
    frames, ln_gain, w_query, keys, values, active, w_out, ffn_gain, w_up, w_down, out,
    fr, lng, ffg, wq, kb, vb, act, wo, wu, wd,
    qown, qb, pb, po, ry, zs, rz, rs, yo, xr, rc, bias, wb,
    ld, s_kv, r_kv, s_fr, r_fr, s_qx, r_qx, s_q, r_q, s_fw, s_yf, r_yf, s_ry, r_ry, s_rz, r_rz,
    s_xa, r_xa, s_xr, r_xr, s_rc, r_rc,
):
    x = lax.axis_index("dp")
    b = lax.axis_index("bank")
    c = lax.rem(b, 2)
    y = lax.rem(b // 2, NY)
    z = b // (2 * NY)

    def dev(dx=0, dz=0, dy=0, core=None):
        cz = lax.rem(z + dz + 2 * NZ, NZ)
        cy = lax.rem(y + dy + NY, NY)
        return (lax.rem(x + dx + NX, NX), (cz * NY + cy) * 2 + (c if core is None else core))

    sibling = dev(core=1 - c)

    def send(src, dst, ssem, rsem, to):
        return pltpu.make_async_remote_copy(
            src_ref=src, dst_ref=dst, send_sem=ssem, recv_sem=rsem, device_id=to, device_id_type=MESH
        )

    def arrived(dst, rsem):
        send(dst, dst, rsem, rsem, sibling).wait_recv()

    def far(i):
        return NEAR[i] + (4 if i % 2 else -4) * c

    loads = [
        pltpu.make_async_copy(src, dst, ld.at[n])
        for n, (src, dst) in enumerate(
            (
                (frames, fr.at[pl.ds(ROWS, ROWS)]),
                (ln_gain, lng),
                (w_query, wq),
                (active, act),
                (keys, kb.at[c]),
                (values, vb.at[c]),
                (w_out, wo),
                (ffn_gain, ffg),
                (w_up, wu),
                (w_down, wd),
            )
        )
    ]
    for load in loads:
        load.start()

    sent, sent0, sent1 = [], [], []

    def finish():
        for copy in sent:
            copy.wait_send()

        @pl.when(c == 0)
        def _():
            for copy in sent0:
                copy.wait_send()

        @pl.when(c == 1)
        def _():
            for copy in sent1:
                copy.wait_send()

    barrier = pltpu.get_barrier_semaphore()

    def greet(to):
        pl.semaphore_signal(barrier, inc=1, device_id=to, device_id_type=MESH)

    @pl.when(c == 1)
    def _():
        for dz in (4, -4, 3, -3, 2, -2, 1, -1):
            greet(dev(dz=dz, core=1))
        for dz in NEAR[::-1] + (-4,):
            greet(dev(dz=-dz, core=0))
        for e in (2, 1, 3):
            greet(dev(dy=e))
            greet(dev(dx=e, core=0))
            greet(dev(dx=e, core=1))

    @pl.when(c == 0)
    def _():
        for dz in NEAR[::-1] + (-4,):
            greet(dev(dz=dz, core=1))
        for e in (2, 1, 3):
            greet(dev(dy=e))
            greet(dev(dx=e, core=1))

    for n in range(4):
        loads[n].wait()
    normed = layer_norm(fr[ROWS:, :], lng[...]).astype(BF16)
    qown[pl.ds(ROWS, ROWS), :] = jnp.dot(normed, wq[...], preferred_element_type=F32).astype(BF16)

    first = (z * NY + y) * 16
    ids = first + lax.broadcasted_iota(jnp.int32, (16, 256), 0)
    hits = jnp.where(ids == act[pl.ds(x, 1), :], 1.0, 0.0).astype(F32)
    found = jnp.max(hits, axis=1, keepdims=True)
    bias[...] = jnp.broadcast_to(jnp.where(found > 0.5, 0.0, -512.0).astype(F32), (16, 128))

    keys_over = send(keys, kb.at[c], s_kv.at[0], r_kv.at[0], sibling)
    values_over = send(values, vb.at[c], s_kv.at[1], r_kv.at[1], sibling)
    query_over = send(qown.at[pl.ds(ROWS, ROWS)], qown.at[pl.ds(0, ROWS)], s_qx, r_qx, sibling)
    frames_over = send(frames, fr.at[pl.ds(0, ROWS)], s_fr, r_fr, sibling)
    def slot(i):
        return qb.at[i // 2, 0, pl.ds((i % 2) * 2 * ROWS, 2 * ROWS)]

    query_out = [send(qown, slot(0), s_q.at[8], r_q.at[0], dev(dz=4, core=1))] + [
        send(qown, slot(i), s_q.at[i], r_q.at[i], dev(dz=-NEAR[i], core=0)) for i in range(7, -1, -1)
    ]
    relay0 = [send(slot(7), slot(i), s_fw.at[i // 2], r_q.at[i], dev(dz=-(i // 2 + 1), core=1)) for i in (7, 5, 3, 1)]
    relay1 = [send(slot(0), slot(i), s_fw.at[i // 2], r_q.at[i], dev(dz=i // 2, core=1)) for i in (6, 4, 2)]

    sent0 += [query_over, frames_over]
    sent0 += relay0
    sent1 += query_out + relay1
    sent += [keys_over, values_over]

    @pl.when(c == 0)
    def _():
        pl.semaphore_wait(barrier, 15)
        query_over.start()

    @pl.when(c == 1)
    def _():
        pl.semaphore_wait(barrier, 26)
        arrived(qown.at[pl.ds(0, ROWS)], r_qx)
        for copy in query_out:
            copy.start()

    keys_over.start()
    values_over.start()

    @pl.when(c == 0)
    def _():
        frames_over.start()

    @pl.when(c == 0)
    def _():
        arrived(slot(7), r_q.at[7])
        for copy in relay0:
            copy.start()
        arrived(slot(0), r_q.at[0])

    @pl.when(c == 1)
    def _():
        arrived(slot(0), r_q.at[0])
        for copy in relay1:
            copy.start()

    for k in range(4):
        for i in (2 * k, 2 * k + 1):
            if 0 < i < 7:
                arrived(slot(i), r_q.at[i])
        if k == 3:

            @pl.when(c == 1)
            def _():
                arrived(slot(7), r_q.at[7])

        for e in (2, 1, 3):
            copy = send(qb.at[k, 0], qb.at[k, NY - e], s_yf.at[k, e - 1], r_yf.at[k, NY - e - 1], dev(dy=e))
            copy.start()
            sent.append(copy)

    for n in range(4, 6):
        loads[n].wait()
    arrived(kb.at[1 - c], r_kv.at[0])
    arrived(vb.at[1 - c], r_kv.at[1])

    def give_back(k, e):
        return send(pb.at[k, e - 1], ry.at[k, NY - e - 1], s_ry.at[k, e - 1], r_ry.at[k, NY - e - 1], dev(dy=e))

    scale = 1.0 / (CAP * BIAS**0.5)

    def attend(k, carry):
        for e in (1, 3, 2):
            arrived(qb.at[k, e], r_yf.at[k, e - 1])
        q = qb[k].reshape(STEP, BIAS)
        tot = jnp.zeros((STEP, 128), F32)
        for p in range(2 * PH // STEP):
            h, at = (p * STEP) // PH, (p * STEP) % PH
            raw = lax.dot_general(
                q, kb[h, pl.ds(at, STEP), :], (((1,), (1,)), ((), ())), preferred_element_type=F32
            )
            off = jnp.concatenate([bias[pl.ds(2 * p, 1), :], bias[pl.ds(2 * p + 1, 1), :]], axis=1)
            weight = jnp.exp2(jnp.tanh(raw * scale) * (CAP * LOG2E) + off)
            tot = tot + (weight[:, :128] + weight[:, 128:])
            wb[:, p * STEP : (p + 1) * STEP] = weight.astype(BF16)
        num = jnp.dot(wb[...], vb[...].reshape(2 * PH, BIAS), preferred_element_type=F32)
        part = 4 * ROWS
        po[k, :, :BIAS] = num[:part]
        po[k, :, BIAS:] = tot[:part]
        for e in (1, 2, 3):
            pb[k, e - 1, :, :BIAS] = num[e * part : (e + 1) * part].astype(BF16)
            pb[k, e - 1, :, BIAS:] = tot[e * part : (e + 1) * part].astype(BF16)
        for e in (2, 1, 3):
            give_back(k, e).start()
        return carry

    lax.fori_loop(0, 4, attend, 0)
    sent += [give_back(k, e) for k in range(4) for e in (1, 2, 3)]

    for k in range(4):
        total = po[k]
        for e in (1, 3, 2):
            arrived(ry.at[k, e - 1], r_ry.at[k, e - 1])
            total = total + ry[k, e - 1].astype(F32)
        zs[k] = total.astype(BF16)
        for j in (1, 0):
            i = 2 * k + j
            copy = send(
                zs.at[k, pl.ds(j * 2 * ROWS, 2 * ROWS)],
                rz.at[c * 8 + i],
                s_rz.at[i],
                r_rz.at[c * 8 + i],
                dev(dz=far(i), core=1),
            )
            copy.start()
            sent.append(copy)

    for n in range(6, 10):
        loads[n].wait()

    residual_out = [
        send(rs.at[0], rs.at[NX - e], s_xa.at[e - 1], r_xa.at[NX - e - 1], dev(dx=e)) for e in (2, 1, 3)
    ]
    residual_over = send(rs.at[0, pl.ds(0, ROWS)], rc, s_rc, r_rc, sibling)
    parts_out = [
        send(
            yo.at[e, pl.ds(core * ROWS, ROWS)],
            xr.at[(NX - e) % NX],
            s_xr.at[e * 2 + core],
            r_xr.at[(NX - e) % NX],
            dev(dx=e, core=core),
        )
        for e, core in ((2, 0), (2, 1), (1, 0), (1, 1), (3, 0), (3, 1), (0, 0))
    ]

    sent1 += residual_out + parts_out + [residual_over]

    @pl.when(c == 1)
    def _():
        arrived(fr.at[pl.ds(0, ROWS)], r_fr)
        total = jnp.zeros((2 * ROWS, WIDE), F32)
        for n in range(16):
            arrived(rz.at[n], r_rz.at[n])
            total = total + rz[n].astype(F32)
        context = total[:, :BIAS] / jnp.sum(total[:, BIAS:], axis=1, keepdims=True)
        power = jnp.mean(context * context, axis=1, keepdims=True)
        context_norm = (context * lax.rsqrt(power + 0.0001)).astype(BF16)
        residual = fr[...].astype(F32) + jnp.dot(context_norm, wo[...], preferred_element_type=F32)
        rs[0] = residual.astype(BF16)
        for copy in residual_out:
            copy.start()
        residual_over.start()
        for e in (1, 3, 2):
            arrived(rs.at[e], r_xa.at[e - 1])
        ffn_in = layer_norm(rs[...].reshape(NX * 2 * ROWS, D), ffg[...]).astype(BF16)
        hidden = gelu(jnp.dot(ffn_in, wu[...], preferred_element_type=F32)).astype(BF16)
        part = jnp.dot(hidden, wd[...], preferred_element_type=F32).astype(BF16)
        yo[...] = part.reshape(NX, 2 * ROWS, D)
        for copy in parts_out:
            copy.start()
        done = rs[0, ROWS:, :].astype(F32) + yo[0, ROWS:, :].astype(F32)
        for e in (1, 3, 2):
            arrived(xr.at[e], r_xr.at[e])
            done = done + xr[e].astype(F32)
        out[...] = done.astype(BF16)

    @pl.when(c == 0)
    def _():
        arrived(rc, r_rc)
        done = rc[...].astype(F32)
        for e in (0, 1, 3, 2):
            arrived(xr.at[e], r_xr.at[e])
            done = done + xr[e].astype(F32)
        out[...] = done.astype(BF16)

    finish()


def local(*args):
    dma = pltpu.SemaphoreType.DMA
    vm = pltpu.VMEM
    rows = 2 * ROWS
    return pl.pallas_call(
        kernel,
        out_shape=jax.ShapeDtypeStruct((ROWS, D), BF16),
        in_specs=[pl.BlockSpec(memory_space=pltpu.HBM)] * 10,
        out_specs=pl.BlockSpec(memory_space=pltpu.VMEM),
        scratch_shapes=[
            vm((rows, D), BF16),
            vm((D,), F32),
            vm((D,), F32),
            vm((D, BIAS), BF16),
            vm((2, PH, BIAS), BF16),
            vm((2, PH, BIAS), BF16),
            vm((4, 256), jnp.int32),
            vm((BIAS, D), BF16),
            vm((D, FFL), BF16),
            vm((FFL, D), BF16),
            vm((rows, BIAS), BF16),
            vm((4, NY, 2 * rows, BIAS), BF16),
            vm((4, 3, 2 * rows, WIDE), BF16),
            vm((4, 2 * rows, WIDE), F32),
            vm((4, 3, 2 * rows, WIDE), BF16),
            vm((4, 2 * rows, WIDE), BF16),
            vm((16, rows, WIDE), BF16),
            vm((NX, rows, D), BF16),
            vm((NX, rows, D), BF16),
            vm((NX, ROWS, D), BF16),
            vm((ROWS, D), BF16),
            vm((16, 128), F32),
            vm((STEP, 2 * PH), BF16),
            dma((10,)),
            dma((2,)), dma((2,)),
            dma, dma,
            dma, dma,
            dma((9,)), dma((8,)), dma((4,)),
            dma((4, 3)), dma((4, 3)),
            dma((4, 3)), dma((4, 3)),
            dma((8,)), dma((16,)),
            dma((3,)), dma((3,)),
            dma((8,)), dma((4,)),
            dma, dma,
        ],
        compiler_params=pltpu.CompilerParams(
            collective_id=0, has_side_effects=True, vmem_limit_bytes=56 * 2**20
        ),
        name="layer",
    )(*args)


def solution(mesh):
    placed = (
        P(("dp", "bank"), None),
        P(),
        P(),
        P("bank", None),
        P("bank", None),
        P(),
        P(),
        P(),
        P(None, "dp"),
        P("dp", None),
    )
    return jax.shard_map(
        local, mesh=mesh, in_specs=placed, out_specs=P(("dp", "bank"), None), check_vma=False
    )
```

```python
import jax
import jax.numpy as jnp
from jax import lax
from jax.experimental import pallas as pl
from jax.experimental.pallas import tpu as pltpu
from jax.sharding import PartitionSpec as P

MESH = pl.DeviceIdType.MESH
F32 = jnp.float32
BF16 = jnp.bfloat16
CAP = 30.0
LOG2E = 1.4426950408889634
NEAR = (0, -1, -2, -3, 1, 2, 3, 4)
NZ, NY, NX = 16, 4, 4
D, FFL, BIAS = 1280, 640, 256
ROWS = 16
PH = 1024
WIDE = BIAS + 128
STEP = 256


def layer_norm(values, gain):
    wide = values.astype(F32)
    center = jnp.mean(wide, axis=-1, keepdims=True)
    moved = wide - center
    spread = jnp.mean(moved * moved, axis=-1, keepdims=True)
    return moved * lax.rsqrt(spread + 1e-05) * gain[None, :]


def gelu(v):
    return 0.5 * v * (1.0 + lax.erf(v * 0.7071067811865476))


def kernel(
    frames, ln_gain, w_query, keys, values, active, w_out, ffn_gain, w_up, w_down, out,
    fr, lng, ffg, wq, kb, vb, act, wo, wu, wd,
    qown, qb, pb, po, ry, zs, rz, cx, rs, yo, xr, rc, bias, wb,
    ld, s_kv, r_kv, s_fr, r_fr, s_qx, r_qx, s_q, r_q, s_fw, s_yf, r_yf, s_ry, r_ry, s_rz, r_rz,
    s_xf, r_xf, s_xa, r_xa, s_xr, r_xr, s_rc, r_rc,
):
    x = lax.axis_index("dp")
    b = lax.axis_index("bank")
    c = lax.rem(b, 2)
    y = lax.rem(b // 2, NY)
    z = b // (2 * NY)
    upper = z // (NZ // 2)

    def dev(dx=0, dz=0, dy=0, core=None):
        cz = lax.rem(z + dz + 2 * NZ, NZ)
        cy = lax.rem(y + dy + NY, NY)
        return (lax.rem(x + dx + NX, NX), (cz * NY + cy) * 2 + (c if core is None else core))

    sibling = dev(core=1 - c)

    def send(src, dst, ssem, rsem, to):
        return pltpu.make_async_remote_copy(
            src_ref=src, dst_ref=dst, send_sem=ssem, recv_sem=rsem, device_id=to, device_id_type=MESH
        )

    def arrived(dst, rsem):
        send(dst, dst, rsem, rsem, sibling).wait_recv()

    loads = [
        pltpu.make_async_copy(src, dst, ld.at[n])
        for n, (src, dst) in enumerate(
            (
                (frames, fr.at[0, pl.ds(ROWS, ROWS)]),
                (ln_gain, lng),
                (w_query, wq),
                (active, act),
                (keys, kb.at[c]),
                (values, vb.at[c]),
                (w_out, wo),
                (ffn_gain, ffg),
                (w_up, wu),
                (w_down, wd),
            )
        )
    ]
    for load in loads:
        load.start()

    sent, sent0, sent1 = [], [], []

    def finish():
        for copy in sent:
            copy.wait_send()

        @pl.when(c == 0)
        def _():
            for copy in sent0:
                copy.wait_send()

        @pl.when(c == 1)
        def _():
            for copy in sent1:
                copy.wait_send()

    barrier = pltpu.get_barrier_semaphore()

    def greet(to):
        pl.semaphore_signal(barrier, inc=1, device_id=to, device_id_type=MESH)

    @pl.when(c == 1)
    def _():
        for dz in (4, -4, 3, -3, 2, -2, 1, -1):
            greet(dev(dz=dz, core=1))
        for dz in (4, -4, 3, -3, 2, -2, 1, -1, 0):
            greet(dev(dz=-dz, core=0))
        for e in (2, 1, 3):
            greet(dev(dy=e))
            greet(dev(dx=e, core=0))
            greet(dev(dx=e, core=1))

    @pl.when(c == 0)
    def _():
        for dz in (4, -4, 3, -3, 2, -2, 1, -1, 0):
            greet(dev(dz=dz, core=1))
        for e in (2, 1, 3):
            greet(dev(dy=e))
            greet(dev(dx=e, core=1))

    for n in range(4):
        loads[n].wait()
    normed = layer_norm(fr[0, ROWS:, :], lng[...]).astype(BF16)
    qown[pl.ds(ROWS, ROWS), :] = jnp.dot(normed, wq[...], preferred_element_type=F32).astype(BF16)

    first = (z * NY + y) * 16
    ids = first + lax.broadcasted_iota(jnp.int32, (16, 256), 0)
    hits = jnp.where(ids == act[pl.ds(x, 1), :], 1.0, 0.0).astype(F32)
    found = jnp.max(hits, axis=1, keepdims=True)
    bias[...] = jnp.broadcast_to(jnp.where(found > 0.5, 0.0, -512.0).astype(F32), (16, 128))

    keys_over = send(keys, kb.at[c], s_kv.at[0], r_kv.at[0], sibling)
    values_over = send(values, vb.at[c], s_kv.at[1], r_kv.at[1], sibling)
    query_over = send(qown.at[pl.ds(ROWS, ROWS)], qown.at[pl.ds(0, ROWS)], s_qx, r_qx, sibling)
    frames_over = send(frames, fr.at[0, pl.ds(0, ROWS)], s_fr, r_fr, sibling)

    def slot(i):
        return qb.at[i // 2, 0, pl.ds((i % 2) * 2 * ROWS, 2 * ROWS)]

    query_out = [send(qown, slot(0), s_q.at[8], r_q.at[0], dev(dz=4, core=1))] + [
        send(qown, slot(i), s_q.at[i], r_q.at[i], dev(dz=-NEAR[i], core=0)) for i in (7, 3, 6, 2, 5, 1, 4, 0)
    ]
    relay0 = [
        send(slot(7), slot(3 + n), s_fw.at[n - 1], r_q.at[3 + n], dev(dz=-n, core=1)) for n in (4, 3, 2, 1)
    ]
    relay1 = [send(slot(0), slot(n), s_fw.at[n - 1], r_q.at[n], dev(dz=n, core=1)) for n in (3, 2, 1)]

    def pass_along():
        @pl.when(c == 0)
        def _():
            arrived(slot(7), r_q.at[7])
            for copy in relay0:
                copy.start()

        @pl.when(c == 1)
        def _():
            arrived(slot(0), r_q.at[0])
            for copy in relay1:
                copy.start()

    def chunk(t):
        return t + upper * (3 - 2 * t)

    def forward(k, e):
        return send(qb.at[k, 0], qb.at[k, NY - e], s_yf.at[k, e - 1], r_yf.at[k, NY - e - 1], dev(dy=e))

    sent0 += [query_over, frames_over]
    sent0 += relay0
    sent1 += query_out + relay1
    sent += [keys_over, values_over]

    @pl.when(c == 0)
    def _():
        pl.semaphore_wait(barrier, 15)
        query_over.start()

    @pl.when(c == 1)
    def _():
        pl.semaphore_wait(barrier, 26)
        arrived(qown.at[pl.ds(0, ROWS)], r_qx)
        for copy in query_out:
            copy.start()

    keys_over.start()
    values_over.start()

    @pl.when(c == 0)
    def _():
        frames_over.start()

    for t in range(4):
        k = chunk(t)
        if t in (0, 2):
            pl.when(c + upper == 1 if t == 0 else c + upper != 1)(pass_along)
        for j in (0, 1):
            held = qb.at[k, 0, pl.ds(j * 2 * ROWS, 2 * ROWS)]
            if t in (1, 2):
                arrived(held, r_q.at[2 * k + j])
            else:

                @pl.when(2 * k + j != 7 - 7 * c)
                def _():
                    arrived(held, r_q.at[2 * k + j])

        for e in (2, 1, 3):
            forward(k, e).start()
    sent += [forward(k, e) for k in range(4) for e in (1, 2, 3)]

    frames_out = [send(fr.at[0], fr.at[NX - e], s_xf.at[e - 1], r_xf.at[NX - e - 1], dev(dx=e)) for e in (2, 1, 3)]
    sent1 += frames_out

    @pl.when(c == 1)
    def _():
        arrived(fr.at[0, pl.ds(0, ROWS)], r_fr)
        for copy in frames_out:
            copy.start()

    for n in range(4, 6):
        loads[n].wait()
    arrived(kb.at[1 - c], r_kv.at[0])
    arrived(vb.at[1 - c], r_kv.at[1])

    def give_back(k, e):
        return send(pb.at[k, e - 1], ry.at[k, NY - e - 1], s_ry.at[k, e - 1], r_ry.at[k, NY - e - 1], dev(dy=e))

    scale = 1.0 / (CAP * BIAS**0.5)

    def to_owner(k, j):
        i = 2 * k + j
        up = i // 4
        distance = up * (i - 3) - (1 - up) * i + (8 * up - 4) * c
        return send(
            zs.at[k, pl.ds(j * 2 * ROWS, 2 * ROWS)],
            rz.at[c * 8 + i],
            s_rz.at[i],
            r_rz.at[c * 8 + i],
            dev(dz=distance, core=1),
        )

    def add_up(t):
        k = chunk(t)
        total = po[k]
        for e in (1, 3, 2):
            arrived(ry.at[k, e - 1], r_ry.at[k, e - 1])
            total = total + ry[k, e - 1].astype(F32)
        zs[k] = total.astype(BF16)
        for j in (1, 0):
            to_owner(k, j).start()

    def attend(t, carry):
        k = chunk(t)
        pl.when(t == 3)(lambda: add_up(0))
        for e in (1, 3, 2):
            arrived(qb.at[k, e], r_yf.at[k, e - 1])
        q = qb[k].reshape(STEP, BIAS)
        tot = jnp.zeros((STEP, 128), F32)
        for p in range(2 * PH // STEP):
            h, at = (p * STEP) // PH, (p * STEP) % PH
            raw = lax.dot_general(
                q, kb[h, pl.ds(at, STEP), :], (((1,), (1,)), ((), ())), preferred_element_type=F32
            )
            off = jnp.concatenate([bias[pl.ds(2 * p, 1), :], bias[pl.ds(2 * p + 1, 1), :]], axis=1)
            weight = jnp.exp2(jnp.tanh(raw * scale) * (CAP * LOG2E) + off)
            tot = tot + (weight[:, :128] + weight[:, 128:])
            wb[:, p * STEP : (p + 1) * STEP] = weight.astype(BF16)
        num = jnp.dot(wb[...], vb[...].reshape(2 * PH, BIAS), preferred_element_type=F32)
        part = 4 * ROWS
        po[k, :, :BIAS] = num[:part]
        po[k, :, BIAS:] = tot[:part]
        for e in (1, 2, 3):
            pb[k, e - 1, :, :BIAS] = num[e * part : (e + 1) * part].astype(BF16)
            pb[k, e - 1, :, BIAS:] = tot[e * part : (e + 1) * part].astype(BF16)
        for e in (2, 1, 3):
            give_back(k, e).start()
        return carry

    lax.fori_loop(0, 4, attend, 0)
    sent += [give_back(k, e) for k in range(4) for e in (1, 2, 3)]

    for t in range(1, 4):
        add_up(t)
    sent += [to_owner(k, j) for k in range(4) for j in (0, 1)]

    for n in range(6, 10):
        loads[n].wait()

    half = D // 2
    context_out = [send(cx.at[0], cx.at[NX - e], s_xa.at[e - 1], r_xa.at[NX - e - 1], dev(dx=e)) for e in (2, 1, 3)]
    residual_over = send(rs.at[0, pl.ds(0, ROWS)], rc, s_rc, r_rc, sibling)
    parts_out = [
        [
            send(
                yo.at[h, e, pl.ds(core * ROWS, ROWS)],
                xr.at[h, (NX - e) % NX],
                s_xr.at[h, e * 2 + core],
                r_xr.at[h, (NX - e) % NX],
                dev(dx=e, core=core),
            )
            for e, core in ((2, 0), (2, 1), (1, 0), (1, 1), (3, 0), (3, 1), (0, 0))
        ]
        for h in (0, 1)
    ]
    sent1 += context_out + parts_out[0] + parts_out[1] + [residual_over]

    @pl.when(c == 1)
    def _():
        for e in (1, 3, 2):
            arrived(fr.at[e], r_xf.at[e - 1])
        total = jnp.zeros((2 * ROWS, WIDE), F32)
        for n in range(16):
            arrived(rz.at[n], r_rz.at[n])
            total = total + rz[n].astype(F32)
        context = total[:, :BIAS] / jnp.sum(total[:, BIAS:], axis=1, keepdims=True)
        power = jnp.mean(context * context, axis=1, keepdims=True)
        cx[0] = (context * lax.rsqrt(power + 0.0001)).astype(BF16)
        for copy in context_out:
            copy.start()
        for e in (1, 3, 2):
            arrived(cx.at[e], r_xa.at[e - 1])
        biased = jnp.dot(cx[...].reshape(NX * 2 * ROWS, BIAS), wo[...], preferred_element_type=F32)
        residual = (fr[...].reshape(NX * 2 * ROWS, D).astype(F32) + biased).astype(BF16)
        rs[...] = residual.reshape(NX, 2 * ROWS, D)
        residual_over.start()
        ffn_in = layer_norm(residual, ffg[...]).astype(BF16)
        hidden = gelu(jnp.dot(ffn_in, wu[...], preferred_element_type=F32)).astype(BF16)
        for h in (0, 1):
            part = jnp.dot(hidden, wd[:, h * half : (h + 1) * half], preferred_element_type=F32)
            yo[h] = part.astype(BF16).reshape(NX, 2 * ROWS, half)
            for copy in parts_out[h]:
                copy.start()
        for h in (0, 1):
            cols = slice(h * half, (h + 1) * half)
            done = rs[0, ROWS:, cols].astype(F32) + yo[h, 0, ROWS:, :].astype(F32)
            for e in (1, 3, 2):
                arrived(xr.at[h, e], r_xr.at[h, e])
                done = done + xr[h, e].astype(F32)
            out[:, cols] = done.astype(BF16)

    @pl.when(c == 0)
    def _():
        arrived(rc, r_rc)
        for h in (0, 1):
            cols = slice(h * half, (h + 1) * half)
            done = rc[:, cols].astype(F32)
            for e in (0, 1, 3, 2):
                arrived(xr.at[h, e], r_xr.at[h, e])
                done = done + xr[h, e].astype(F32)
            out[:, cols] = done.astype(BF16)

    finish()


def local(*args):
    dma = pltpu.SemaphoreType.DMA
    vm = pltpu.VMEM
    rows = 2 * ROWS
    return pl.pallas_call(
        kernel,
        out_shape=jax.ShapeDtypeStruct((ROWS, D), BF16),
        in_specs=[pl.BlockSpec(memory_space=pltpu.HBM)] * 10,
        out_specs=pl.BlockSpec(memory_space=pltpu.VMEM),
        scratch_shapes=[
            vm((NX, rows, D), BF16),
            vm((D,), F32),
            vm((D,), F32),
            vm((D, BIAS), BF16),
            vm((2, PH, BIAS), BF16),
            vm((2, PH, BIAS), BF16),
            vm((4, 256), jnp.int32),
            vm((BIAS, D), BF16),
            vm((D, FFL), BF16),
            vm((FFL, D), BF16),
            vm((rows, BIAS), BF16),
            vm((4, NY, 2 * rows, BIAS), BF16),
            vm((4, 3, 2 * rows, WIDE), BF16),
            vm((4, 2 * rows, WIDE), F32),
            vm((4, 3, 2 * rows, WIDE), BF16),
            vm((4, 2 * rows, WIDE), BF16),
            vm((16, rows, WIDE), BF16),
            vm((NX, rows, BIAS), BF16),
            vm((NX, rows, D), BF16),
            vm((2, NX, rows, D // 2), BF16),
            vm((2, NX, ROWS, D // 2), BF16),
            vm((ROWS, D), BF16),
            vm((16, 128), F32),
            vm((STEP, 2 * PH), BF16),
            dma((10,)),
            dma((2,)), dma((2,)),
            dma, dma,
            dma, dma,
            dma((9,)), dma((8,)), dma((4,)),
            dma((4, 3)), dma((4, 3)),
            dma((4, 3)), dma((4, 3)),
            dma((8,)), dma((16,)),
            dma((3,)), dma((3,)),
            dma((3,)), dma((3,)),
            dma((2, 8)), dma((2, 4)),
            dma, dma,
        ],
        compiler_params=pltpu.CompilerParams(
            collective_id=0, has_side_effects=True, vmem_limit_bytes=56 * 2**20
        ),
        name="layer",
    )(*args)


def solution(mesh):
    placed = (
        P(("dp", "bank"), None),
        P(),
        P(),
        P("bank", None),
        P("bank", None),
        P(),
        P(),
        P(),
        P(None, "dp"),
        P("dp", None),
    )
    return jax.shard_map(
        local, mesh=mesh, in_specs=placed, out_specs=P(("dp", "bank"), None), check_vma=False
    )
```

```python
import jax
import jax.numpy as jnp
from jax import lax
from jax.experimental import pallas as pl
from jax.experimental.pallas import tpu as pltpu
from jax.sharding import PartitionSpec as P

MESH = pl.DeviceIdType.MESH
F32 = jnp.float32
BF16 = jnp.bfloat16
CAP = 30.0
LOG2E = 1.4426950408889634
NEAR = (0, -1, -2, -3, 1, 2, 3, 4)
NZ, NY, NX = 16, 4, 4
D, FFL, BIAS = 1280, 640, 256
ROWS = 16
PH = 1024
STEP = 256


def layer_norm(values, gain):
    wide = values.astype(F32)
    center = jnp.mean(wide, axis=-1, keepdims=True)
    moved = wide - center
    spread = jnp.mean(moved * moved, axis=-1, keepdims=True)
    return moved * lax.rsqrt(spread + 1e-05) * gain[None, :]


def gelu(v):
    return 0.5 * v * (1.0 + lax.erf(v * 0.7071067811865476))


def kernel(
    frames, ln_gain, w_query, keys, values, active, w_out, ffn_gain, w_up, w_down, out,
    fr, lng, ffg, wq, kb, vb, act, wo, wu, wd,
    qown, qb, pb, po, ry, zs, rz, ty, tr, ts, tz, cx, rs, yo, xr, rc, bias, wb,
    ld, s_kv, r_kv, s_fr, r_fr, s_qx, r_qx, s_q, r_q, s_fw, s_yf, r_yf, s_ry, r_ry, s_rz, r_rz,
    s_ty, r_ty, s_tz, r_tz, s_xf, r_xf, s_xa, r_xa, s_xr, r_xr, s_rc, r_rc,
):
    x = lax.axis_index("dp")
    b = lax.axis_index("bank")
    c = lax.rem(b, 2)
    y = lax.rem(b // 2, NY)
    z = b // (2 * NY)
    upper = z // (NZ // 2)

    def dev(dx=0, dz=0, dy=0, core=None):
        cz = lax.rem(z + dz + 2 * NZ, NZ)
        cy = lax.rem(y + dy + NY, NY)
        return (lax.rem(x + dx + NX, NX), (cz * NY + cy) * 2 + (c if core is None else core))

    sibling = dev(core=1 - c)

    def send(src, dst, ssem, rsem, to):
        return pltpu.make_async_remote_copy(
            src_ref=src, dst_ref=dst, send_sem=ssem, recv_sem=rsem, device_id=to, device_id_type=MESH
        )

    def arrived(dst, rsem):
        send(dst, dst, rsem, rsem, sibling).wait_recv()

    loads = [
        pltpu.make_async_copy(src, dst, ld.at[n])
        for n, (src, dst) in enumerate(
            (
                (frames, fr.at[0, pl.ds(ROWS, ROWS)]),
                (ln_gain, lng),
                (w_query, wq),
                (active, act),
                (keys, kb.at[c]),
                (values, vb.at[c]),
                (w_out, wo),
                (ffn_gain, ffg),
                (w_up, wu),
                (w_down, wd),
            )
        )
    ]
    for load in loads:
        load.start()

    sent, sent0, sent1 = [], [], []

    def finish():
        for copy in sent:
            copy.wait_send()

        @pl.when(c == 0)
        def _():
            for copy in sent0:
                copy.wait_send()

        @pl.when(c == 1)
        def _():
            for copy in sent1:
                copy.wait_send()

    barrier = pltpu.get_barrier_semaphore()

    def greet(to):
        pl.semaphore_signal(barrier, inc=1, device_id=to, device_id_type=MESH)

    @pl.when(c == 1)
    def _():
        for dz in (4, -4, 3, -3, 2, -2, 1, -1):
            greet(dev(dz=dz, core=1))
        for dz in (4, -4, 3, -3, 2, -2, 1, -1, 0):
            greet(dev(dz=-dz, core=0))
        for e in (2, 1, 3):
            greet(dev(dy=e))
            greet(dev(dx=e, core=0))
            greet(dev(dx=e, core=1))

    @pl.when(c == 0)
    def _():
        for dz in (4, -4, 3, -3, 2, -2, 1, -1, 0):
            greet(dev(dz=dz, core=1))
        for e in (2, 1, 3):
            greet(dev(dy=e))
            greet(dev(dx=e, core=1))

    for n in range(4):
        loads[n].wait()
    normed = layer_norm(fr[0, ROWS:, :], lng[...]).astype(BF16)
    qown[pl.ds(ROWS, ROWS), :] = jnp.dot(normed, wq[...], preferred_element_type=F32).astype(BF16)

    first = (z * NY + y) * 16
    ids = first + lax.broadcasted_iota(jnp.int32, (16, 256), 0)
    hits = jnp.where(ids == act[pl.ds(x, 1), :], 1.0, 0.0).astype(F32)
    found = jnp.max(hits, axis=1, keepdims=True)
    ty[...] = jnp.zeros_like(ty)
    bias[...] = jnp.broadcast_to(jnp.where(found > 0.5, 0.0, -512.0).astype(F32), (16, 128))

    keys_over = send(keys, kb.at[c], s_kv.at[0], r_kv.at[0], sibling)
    values_over = send(values, vb.at[c], s_kv.at[1], r_kv.at[1], sibling)
    query_over = send(qown.at[pl.ds(ROWS, ROWS)], qown.at[pl.ds(0, ROWS)], s_qx, r_qx, sibling)
    frames_over = send(frames, fr.at[0, pl.ds(0, ROWS)], s_fr, r_fr, sibling)

    def slot(i):
        return qb.at[i // 2, 0, pl.ds((i % 2) * 2 * ROWS, 2 * ROWS)]

    query_out = [send(qown, slot(0), s_q.at[8], r_q.at[0], dev(dz=4, core=1))] + [
        send(qown, slot(i), s_q.at[i], r_q.at[i], dev(dz=-NEAR[i], core=0)) for i in (7, 3, 6, 2, 5, 1, 4, 0)
    ]
    relay0 = [
        send(slot(7), slot(3 + n), s_fw.at[n - 1], r_q.at[3 + n], dev(dz=-n, core=1)) for n in (4, 3, 2, 1)
    ]
    relay1 = [send(slot(0), slot(n), s_fw.at[n - 1], r_q.at[n], dev(dz=n, core=1)) for n in (3, 2, 1)]

    def pass_along():
        @pl.when(c == 0)
        def _():
            arrived(slot(7), r_q.at[7])
            for copy in relay0:
                copy.start()

        @pl.when(c == 1)
        def _():
            arrived(slot(0), r_q.at[0])
            for copy in relay1:
                copy.start()

    def chunk(t):
        return t + upper * (3 - 2 * t)

    def forward(k, e):
        return send(qb.at[k, 0], qb.at[k, NY - e], s_yf.at[k, e - 1], r_yf.at[k, NY - e - 1], dev(dy=e))

    sent0 += [query_over, frames_over]
    sent0 += relay0
    sent1 += query_out + relay1
    sent += [keys_over, values_over]

    @pl.when(c == 0)
    def _():
        pl.semaphore_wait(barrier, 15)
        query_over.start()

    @pl.when(c == 1)
    def _():
        pl.semaphore_wait(barrier, 26)
        arrived(qown.at[pl.ds(0, ROWS)], r_qx)
        for copy in query_out:
            copy.start()

    keys_over.start()
    values_over.start()

    @pl.when(c == 0)
    def _():
        frames_over.start()

    for t in range(4):
        k = chunk(t)
        if t in (0, 2):
            pl.when(c + upper == 1 if t == 0 else c + upper != 1)(pass_along)
        for j in (0, 1):
            held = qb.at[k, 0, pl.ds(j * 2 * ROWS, 2 * ROWS)]
            if t in (1, 2):
                arrived(held, r_q.at[2 * k + j])
            else:

                @pl.when(2 * k + j != 7 - 7 * c)
                def _():
                    arrived(held, r_q.at[2 * k + j])

        for e in (2, 1, 3):
            forward(k, e).start()
    sent += [forward(k, e) for k in range(4) for e in (1, 2, 3)]

    frames_out = [send(fr.at[0], fr.at[NX - e], s_xf.at[e - 1], r_xf.at[NX - e - 1], dev(dx=e)) for e in (2, 1, 3)]
    sent1 += frames_out

    @pl.when(c == 1)
    def _():
        arrived(fr.at[0, pl.ds(0, ROWS)], r_fr)
        for copy in frames_out:
            copy.start()

    for n in range(4, 6):
        loads[n].wait()
    arrived(kb.at[1 - c], r_kv.at[0])
    arrived(vb.at[1 - c], r_kv.at[1])

    def give_back(k, e):
        return send(pb.at[k, e - 1], ry.at[k, NY - e - 1], s_ry.at[k, e - 1], r_ry.at[k, NY - e - 1], dev(dy=e))

    scale = 1.0 / (CAP * BIAS**0.5)

    def to_owner(k, j):
        i = 2 * k + j
        up = i // 4
        distance = up * (i - 3) - (1 - up) * i + (8 * up - 4) * c
        return send(
            zs.at[k, pl.ds(j * 2 * ROWS, 2 * ROWS)],
            rz.at[c * 8 + i],
            s_rz.at[i],
            r_rz.at[c * 8 + i],
            dev(dz=distance, core=1),
        )

    def add_up(t):
        k = chunk(t)
        total = po[k]
        for e in (1, 3, 2):
            arrived(ry.at[k, e - 1], r_ry.at[k, e - 1])
            total = total + ry[k, e - 1].astype(F32)
        zs[k] = total.astype(BF16)
        for j in (1, 0):
            to_owner(k, j).start()

    def attend(t, carry):
        k = chunk(t)
        pl.when(t == 3)(lambda: add_up(0))
        for e in (1, 3, 2):
            arrived(qb.at[k, e], r_yf.at[k, e - 1])
        q = qb[k].reshape(STEP, BIAS)
        tot = jnp.zeros((STEP, 128), F32)
        for p in range(2 * PH // STEP):
            h, at = (p * STEP) // PH, (p * STEP) % PH
            raw = lax.dot_general(
                q, kb[h, pl.ds(at, STEP), :], (((1,), (1,)), ((), ())), preferred_element_type=F32
            )
            off = jnp.concatenate([bias[pl.ds(2 * p, 1), :], bias[pl.ds(2 * p + 1, 1), :]], axis=1)
            weight = jnp.exp2(jnp.tanh(raw * scale) * (CAP * LOG2E) + off)
            tot = tot + (weight[:, :128] + weight[:, 128:])
            wb[:, p * STEP : (p + 1) * STEP] = weight.astype(BF16)
        num = jnp.dot(wb[...], vb[...].reshape(2 * PH, BIAS), preferred_element_type=F32)
        part = 4 * ROWS
        po[k] = num[:part]
        for e in (2, 1, 3):
            pb[k, e - 1] = num[e * part : (e + 1) * part].astype(BF16)
            give_back(k, e).start()
        row = lax.dot_general(
            jnp.ones((8, 128), BF16), tot.astype(BF16), (((1,), (1,)), ((), ())), preferred_element_type=F32
        )
        for e in range(NY):
            ty[e, k, :, :part] = row[:1, e * part : (e + 1) * part]
        return carry

    lax.fori_loop(0, 4, attend, 0)
    sent += [give_back(k, e) for k in range(4) for e in (1, 2, 3)]

    totals_back = [send(ty.at[e], tr.at[NY - e - 1], s_ty.at[e - 1], r_ty.at[NY - e - 1], dev(dy=e)) for e in (2, 1, 3)]
    for copy in totals_back:
        copy.start()
    sent += totals_back

    for t in range(1, 4):
        add_up(t)
    totals = ty[0]
    for e in (1, 3, 2):
        arrived(tr.at[e - 1], r_ty.at[e - 1])
        totals = totals + tr[e - 1]
    ts[...] = totals
    totals_out = [
        send(ts.at[i // 2], tz.at[c * 8 + i], s_tz.at[i], r_tz, dev(dz=NEAR[i] + (-4 if i < 4 else 4) * c, core=1))
        for i in (7, 3, 6, 2, 5, 1, 4, 0)
    ]
    for copy in totals_out:
        copy.start()
    sent += totals_out
    sent += [to_owner(k, j) for k in range(4) for j in (0, 1)]

    for n in range(6, 10):
        loads[n].wait()

    half = D // 2
    context_out = [send(cx.at[0], cx.at[NX - e], s_xa.at[e - 1], r_xa.at[NX - e - 1], dev(dx=e)) for e in (2, 1, 3)]
    residual_over = send(rs.at[0, pl.ds(0, ROWS)], rc, s_rc, r_rc, sibling)
    parts_out = [
        [
            send(
                yo.at[h, e, pl.ds(core * ROWS, ROWS)],
                xr.at[h, (NX - e) % NX],
                s_xr.at[h, e * 2 + core],
                r_xr.at[h, (NX - e) % NX],
                dev(dx=e, core=core),
            )
            for e, core in ((2, 0), (2, 1), (1, 0), (1, 1), (3, 0), (3, 1), (0, 0))
        ]
        for h in (0, 1)
    ]
    sent1 += context_out + parts_out[0] + parts_out[1] + [residual_over]

    @pl.when(c == 1)
    def _():
        for e in (1, 3, 2):
            arrived(fr.at[e], r_xf.at[e - 1])
        total = jnp.zeros((2 * ROWS, BIAS), F32)
        for n in range(16):
            arrived(rz.at[n], r_rz.at[n])
            total = total + rz[n].astype(F32)
        arrived(tz, r_tz)
        even, odd = tz[0], tz[1]
        for n in range(2, 16, 2):
            even, odd = even + tz[n], odd + tz[n + 1]
        gap = lax.broadcasted_iota(jnp.int32, (2 * ROWS, 128), 1) - lax.broadcasted_iota(jnp.int32, (2 * ROWS, 128), 0)
        spread = jnp.where(gap == 0, even, 0.0) + jnp.where(gap == 2 * ROWS, odd, 0.0)
        context = total / jnp.sum(spread, axis=1, keepdims=True)
        power = jnp.mean(context * context, axis=1, keepdims=True)
        cx[0] = (context * lax.rsqrt(power + 0.0001)).astype(BF16)
        for copy in context_out:
            copy.start()
        for e in (1, 3, 2):
            arrived(cx.at[e], r_xa.at[e - 1])
        biased = jnp.dot(cx[...].reshape(NX * 2 * ROWS, BIAS), wo[...], preferred_element_type=F32)
        residual = (fr[...].reshape(NX * 2 * ROWS, D).astype(F32) + biased).astype(BF16)
        rs[...] = residual.reshape(NX, 2 * ROWS, D)
        residual_over.start()
        ffn_in = layer_norm(residual, ffg[...]).astype(BF16)
        hidden = gelu(jnp.dot(ffn_in, wu[...], preferred_element_type=F32)).astype(BF16)
        for h in (0, 1):
            part = jnp.dot(hidden, wd[:, h * half : (h + 1) * half], preferred_element_type=F32)
            yo[h] = part.astype(BF16).reshape(NX, 2 * ROWS, half)
            for copy in parts_out[h]:
                copy.start()
        for h in (0, 1):
            cols = slice(h * half, (h + 1) * half)
            done = rs[0, ROWS:, cols].astype(F32) + yo[h, 0, ROWS:, :].astype(F32)
            for e in (1, 3, 2):
                arrived(xr.at[h, e], r_xr.at[h, e])
                done = done + xr[h, e].astype(F32)
            out[:, cols] = done.astype(BF16)

    @pl.when(c == 0)
    def _():
        arrived(rc, r_rc)
        for h in (0, 1):
            cols = slice(h * half, (h + 1) * half)
            done = rc[:, cols].astype(F32)
            for e in (0, 1, 3, 2):
                arrived(xr.at[h, e], r_xr.at[h, e])
                done = done + xr[h, e].astype(F32)
            out[:, cols] = done.astype(BF16)

    finish()


def local(*args):
    dma = pltpu.SemaphoreType.DMA
    vm = pltpu.VMEM
    rows = 2 * ROWS
    return pl.pallas_call(
        kernel,
        out_shape=jax.ShapeDtypeStruct((ROWS, D), BF16),
        in_specs=[pl.BlockSpec(memory_space=pltpu.HBM)] * 10,
        out_specs=pl.BlockSpec(memory_space=pltpu.VMEM),
        scratch_shapes=[
            vm((NX, rows, D), BF16),
            vm((D,), F32),
            vm((D,), F32),
            vm((D, BIAS), BF16),
            vm((2, PH, BIAS), BF16),
            vm((2, PH, BIAS), BF16),
            vm((4, 256), jnp.int32),
            vm((BIAS, D), BF16),
            vm((D, FFL), BF16),
            vm((FFL, D), BF16),
            vm((rows, BIAS), BF16),
            vm((4, NY, 2 * rows, BIAS), BF16),
            vm((4, 3, 2 * rows, BIAS), BF16),
            vm((4, 2 * rows, BIAS), F32),
            vm((4, 3, 2 * rows, BIAS), BF16),
            vm((4, 2 * rows, BIAS), BF16),
            vm((16, rows, BIAS), BF16),
            vm((NY, 4, 1, 128), F32),
            vm((3, 4, 1, 128), F32),
            vm((4, 1, 128), F32),
            vm((16, 1, 128), F32),
            vm((NX, rows, BIAS), BF16),
            vm((NX, rows, D), BF16),
            vm((2, NX, rows, D // 2), BF16),
            vm((2, NX, ROWS, D // 2), BF16),
            vm((ROWS, D), BF16),
            vm((16, 128), F32),
            vm((STEP, 2 * PH), BF16),
            dma((10,)),
            dma((2,)), dma((2,)),
            dma, dma,
            dma, dma,
            dma((9,)), dma((8,)), dma((4,)),
            dma((4, 3)), dma((4, 3)),
            dma((4, 3)), dma((4, 3)),
            dma((8,)), dma((16,)),
            dma((3,)), dma((3,)),
            dma((8,)), dma,
            dma((3,)), dma((3,)),
            dma((3,)), dma((3,)),
            dma((2, 8)), dma((2, 4)),
            dma, dma,
        ],
        compiler_params=pltpu.CompilerParams(
            collective_id=0, has_side_effects=True, vmem_limit_bytes=56 * 2**20
        ),
        name="layer",
    )(*args)


def solution(mesh):
    placed = (
        P(("dp", "bank"), None),
        P(),
        P(),
        P("bank", None),
        P("bank", None),
        P(),
        P(),
        P(),
        P(None, "dp"),
        P("dp", None),
    )
    return jax.shard_map(
        local, mesh=mesh, in_specs=placed, out_specs=P(("dp", "bank"), None), check_vma=False
    )
```

```python
import jax
import jax.numpy as jnp
from jax import lax
from jax.experimental import pallas as pl
from jax.experimental.pallas import tpu as pltpu
from jax.sharding import PartitionSpec as P

MESH = pl.DeviceIdType.MESH
F32 = jnp.float32
BF16 = jnp.bfloat16
CAP = 30.0
LOG2E = 1.4426950408889634
NEAR = (0, 1, -1, 2, -2, 3, -3, 4)
FAR = (-4, 5, -5, 6, -6, 7, -7, 8)
NZ, NY, NX = 16, 4, 4
D, FFL, BIAS = 1280, 640, 256
ROWS = 16
PH = 1024
STEP = 256


def layer_norm(values, gain):
    wide = values.astype(F32)
    center = jnp.mean(wide, axis=-1, keepdims=True)
    moved = wide - center
    spread = jnp.mean(moved * moved, axis=-1, keepdims=True)
    return moved * lax.rsqrt(spread + 1e-05) * gain[None, :]


def gelu(v):
    return 0.5 * v * (1.0 + lax.erf(v * 0.7071067811865476))


def kernel(
    frames, ln_gain, w_query, keys, values, active, w_out, ffn_gain, w_up, w_down, out,
    fr, lng, ffg, wq, kb, vb, act, wo, wu, wd,
    qown, qb, pb, po, ry, zs, rz, ty, tr, ts, tz, cx, rs, yo, xr, rc, bias, wb, upper,
    ld, s_kv, r_kv, s_fr, r_fr, s_qx, r_qx, s_q, r_q, r_up, s_fw, s_yf, r_yf, s_ry, r_ry, s_rz, r_rz,
    s_ty, r_ty, s_tz, r_tz, s_xf, r_xf, s_xa, r_xa, s_xr, r_xr, s_rc, r_rc,
):
    x = lax.axis_index("dp")
    b = lax.axis_index("bank")
    c = lax.rem(b, 2)
    y = lax.rem(b // 2, NY)
    z = b // (2 * NY)

    def dev(dx=0, dz=0, dy=0, core=None):
        cz = lax.rem(z + dz + 2 * NZ, NZ)
        cy = lax.rem(y + dy + NY, NY)
        return (lax.rem(x + dx + NX, NX), (cz * NY + cy) * 2 + (c if core is None else core))

    sibling = dev(core=1 - c)

    def send(src, dst, ssem, rsem, to):
        return pltpu.make_async_remote_copy(
            src_ref=src, dst_ref=dst, send_sem=ssem, recv_sem=rsem, device_id=to, device_id_type=MESH
        )

    def arrived(dst, rsem):
        send(dst, dst, rsem, rsem, sibling).wait_recv()

    loads = [
        pltpu.make_async_copy(src, dst, ld.at[n])
        for n, (src, dst) in enumerate(
            (
                (frames, fr.at[0, pl.ds(ROWS, ROWS)]),
                (ln_gain, lng),
                (w_query, wq),
                (active, act),
                (keys, kb.at[c]),
                (values, vb.at[c]),
                (w_out, wo),
                (ffn_gain, ffg),
                (w_up, wu),
                (w_down, wd),
            )
        )
    ]
    for load in loads[:4]:
        load.start()

    sent, sent0, sent1 = [], [], []

    def finish():
        for copy in sent:
            copy.wait_send()

        @pl.when(c == 0)
        def _():
            for copy in sent0:
                copy.wait_send()

        @pl.when(c == 1)
        def _():
            for copy in sent1:
                copy.wait_send()

    barrier = pltpu.get_barrier_semaphore()

    def greet(to):
        pl.semaphore_signal(barrier, inc=1, device_id=to, device_id_type=MESH)

    @pl.when(c == 1)
    def _():
        for dz in (4, -4, 3, -3, 2, -2, 1, -1):
            greet(dev(dz=dz, core=1))
        for dz in NEAR[::-1]:
            greet(dev(dz=-dz, core=0))
        for e in (2, 1, 3):
            greet(dev(dy=e))
            greet(dev(dx=e, core=0))
            greet(dev(dx=e, core=1))

    @pl.when(c == 0)
    def _():
        for dz in NEAR[::-1]:
            greet(dev(dz=dz, core=1))
        for e in (2, 1, 3):
            greet(dev(dy=e))
            greet(dev(dx=e, core=1))

    for n in range(4):
        loads[n].wait()
    for load in loads[4:]:
        load.start()
    normed = layer_norm(fr[0, ROWS:, :], lng[...]).astype(BF16)
    qown[pl.ds(ROWS, ROWS), :] = jnp.dot(normed, wq[...], preferred_element_type=F32).astype(BF16)

    first = (z * NY + y) * 16
    ids = first + lax.broadcasted_iota(jnp.int32, (16, 256), 0)
    hits = jnp.where(ids == act[pl.ds(x, 1), :], 1.0, 0.0).astype(F32)
    found = jnp.max(hits, axis=1, keepdims=True)
    ty[...] = jnp.zeros_like(ty)
    bias[...] = jnp.broadcast_to(jnp.where(found > 0.5, 0.0, -512.0).astype(F32), (16, 128))

    keys_over = send(keys, kb.at[c], s_kv.at[0], r_kv.at[0], sibling)
    values_over = send(values, vb.at[c], s_kv.at[1], r_kv.at[1], sibling)
    query_over = send(qown.at[pl.ds(ROWS, ROWS)], qown.at[pl.ds(0, ROWS)], s_qx, r_qx, sibling)
    frames_over = send(frames, fr.at[0, pl.ds(0, ROWS)], s_fr, r_fr, sibling)

    def slot(i):
        return qb.at[i // 2, 0, pl.ds((i % 2) * 2 * ROWS, 2 * ROWS)]

    query_out = [
        send(qown, upper, s_q.at[9], r_up, dev(dz=-4, core=1)),
        send(qown, slot(0), s_q.at[8], r_q.at[0], dev(dz=4, core=1)),
    ] + [
        send(qown, slot(i), s_q.at[i], r_q.at[i], dev(dz=-NEAR[i], core=0)) for i in range(7, -1, -1)
    ]
    relay_down = [
        send(upper, slot(2 * n - 1), s_fw.at[2 * n - 1], r_q.at[2 * n - 1], dev(dz=-n, core=1)) for n in (4, 3, 2, 1)
    ]
    relay_up = [send(slot(0), slot(2 * n), s_fw.at[2 * n], r_q.at[2 * n], dev(dz=n, core=1)) for n in (3, 2, 1)]

    def forward(k, e):
        return send(qb.at[k, 0], qb.at[k, NY - e], s_yf.at[k, e - 1], r_yf.at[k, NY - e - 1], dev(dy=e))

    sent0 += [query_over, frames_over]
    sent1 += query_out + relay_down + relay_up
    sent += [keys_over, values_over]

    @pl.when(c == 0)
    def _():
        pl.semaphore_wait(barrier, 14)
        query_over.start()

    @pl.when(c == 1)
    def _():
        pl.semaphore_wait(barrier, 25)
        arrived(qown.at[pl.ds(0, ROWS)], r_qx)
        for copy in query_out:
            copy.start()

    keys_over.start()
    values_over.start()

    @pl.when(c == 0)
    def _():
        frames_over.start()

    @pl.when(c == 1)
    def _():
        arrived(upper, r_up)
        for copy in relay_down:
            copy.start()

    arrived(slot(0), r_q.at[0])

    @pl.when(c == 1)
    def _():
        for copy in relay_up:
            copy.start()

    for k in range(4):
        for i in (2 * k, 2 * k + 1):
            if i:
                arrived(slot(i), r_q.at[i])
        for e in (2, 1, 3):
            forward(k, e).start()
    sent += [forward(k, e) for k in range(4) for e in (1, 2, 3)]

    frames_out = [send(fr.at[0], fr.at[NX - e], s_xf.at[e - 1], r_xf.at[NX - e - 1], dev(dx=e)) for e in (2, 1, 3)]
    sent1 += frames_out

    @pl.when(c == 1)
    def _():
        arrived(fr.at[0, pl.ds(0, ROWS)], r_fr)
        for copy in frames_out:
            copy.start()

    for n in range(4, 6):
        loads[n].wait()
    arrived(kb.at[1 - c], r_kv.at[0])
    arrived(vb.at[1 - c], r_kv.at[1])

    def give_back(k, e):
        return send(pb.at[k, e - 1], ry.at[k, NY - e - 1], s_ry.at[k, e - 1], r_ry.at[k, NY - e - 1], dev(dy=e))

    scale = 1.0 / (CAP * BIAS**0.5)

    def owner(i):
        return dev(dz=NEAR[i] + (FAR[i] - NEAR[i]) * c, core=1)

    def to_owner(k, j):
        i = 2 * k + j
        return send(
            zs.at[k, pl.ds(j * 2 * ROWS, 2 * ROWS)], rz.at[c * 8 + i], s_rz.at[i], r_rz.at[c * 8 + i], owner(i)
        )

    def add_up(k):
        total = po[k]
        for e in (1, 3, 2):
            arrived(ry.at[k, e - 1], r_ry.at[k, e - 1])
            total = total + ry[k, e - 1].astype(F32)
        zs[k] = total.astype(BF16)
        for j in (1, 0):
            to_owner(k, j).start()

    def attend(k, carry):
        pl.when((k == 3) & (c == 0))(lambda: add_up(0))
        for e in (1, 3, 2):
            arrived(qb.at[k, e], r_yf.at[k, e - 1])
        q = qb[k].reshape(STEP, BIAS)
        tot = jnp.zeros((STEP, 128), F32)
        for p in range(2 * PH // STEP):
            h, at = (p * STEP) // PH, (p * STEP) % PH
            raw = lax.dot_general(
                q, kb[h, pl.ds(at, STEP), :], (((1,), (1,)), ((), ())), preferred_element_type=F32
            )
            off = jnp.concatenate([bias[pl.ds(2 * p, 1), :], bias[pl.ds(2 * p + 1, 1), :]], axis=1)
            weight = jnp.exp2(jnp.tanh(raw * scale) * (CAP * LOG2E) + off)
            tot = tot + (weight[:, :128] + weight[:, 128:])
            wb[:, p * STEP : (p + 1) * STEP] = weight.astype(BF16)
        num = jnp.dot(wb[...], vb[...].reshape(2 * PH, BIAS), preferred_element_type=F32)
        part = 4 * ROWS
        po[k] = num[:part]
        for e in (2, 1, 3):
            pb[k, e - 1] = num[e * part : (e + 1) * part].astype(BF16)
            give_back(k, e).start()
        row = lax.dot_general(
            jnp.ones((8, 128), BF16), tot.astype(BF16), (((1,), (1,)), ((), ())), preferred_element_type=F32
        )
        for e in range(NY):
            ty[e, k, :, :part] = row[:1, e * part : (e + 1) * part]
        return carry

    lax.fori_loop(0, 4, attend, 0)
    sent += [give_back(k, e) for k in range(4) for e in (1, 2, 3)]

    totals_back = [send(ty.at[e], tr.at[NY - e - 1], s_ty.at[e - 1], r_ty.at[NY - e - 1], dev(dy=e)) for e in (2, 1, 3)]
    for copy in totals_back:
        copy.start()
    sent += totals_back

    pl.when(c == 1)(lambda: add_up(0))
    for k in range(1, 4):
        add_up(k)
    totals = ty[0]
    for e in (1, 3, 2):
        arrived(tr.at[e - 1], r_ty.at[e - 1])
        totals = totals + tr[e - 1]
    ts[...] = totals
    totals_out = [
        send(ts.at[i // 2], tz.at[c * 8 + i], s_tz.at[i], r_tz, owner(i))
        for i in range(7, -1, -1)
    ]
    for copy in totals_out:
        copy.start()
    sent += totals_out
    sent += [to_owner(k, j) for k in range(4) for j in (0, 1)]

    for n in range(6, 10):
        loads[n].wait()

    half = D // 2
    context_out = [send(cx.at[0], cx.at[NX - e], s_xa.at[e - 1], r_xa.at[NX - e - 1], dev(dx=e)) for e in (2, 1, 3)]
    residual_over = send(rs.at[0, pl.ds(0, ROWS)], rc, s_rc, r_rc, sibling)
    parts_out = [
        [
            send(
                yo.at[h, e, pl.ds(core * ROWS, ROWS)],
                xr.at[h, (NX - e) % NX],
                s_xr.at[h, e * 2 + core],
                r_xr.at[h, (NX - e) % NX],
                dev(dx=e, core=core),
            )
            for e, core in ((2, 0), (2, 1), (1, 0), (1, 1), (3, 0), (3, 1), (0, 0))
        ]
        for h in (0, 1)
    ]
    sent1 += context_out + parts_out[0] + parts_out[1] + [residual_over]

    @pl.when(c == 1)
    def _():
        for e in (1, 3, 2):
            arrived(fr.at[e], r_xf.at[e - 1])
        total = jnp.zeros((2 * ROWS, BIAS), F32)
        for n in range(16):
            arrived(rz.at[n], r_rz.at[n])
            total = total + rz[n].astype(F32)
        arrived(tz, r_tz)
        even, odd = tz[0], tz[1]
        for n in range(2, 16, 2):
            even, odd = even + tz[n], odd + tz[n + 1]
        gap = lax.broadcasted_iota(jnp.int32, (2 * ROWS, 128), 1) - lax.broadcasted_iota(jnp.int32, (2 * ROWS, 128), 0)
        spread = jnp.where(gap == 0, even, 0.0) + jnp.where(gap == 2 * ROWS, odd, 0.0)
        context = total / jnp.sum(spread, axis=1, keepdims=True)
        power = jnp.mean(context * context, axis=1, keepdims=True)
        cx[0] = (context * lax.rsqrt(power + 0.0001)).astype(BF16)
        for copy in context_out:
            copy.start()
        for e in (1, 3, 2):
            arrived(cx.at[e], r_xa.at[e - 1])
        biased = jnp.dot(cx[...].reshape(NX * 2 * ROWS, BIAS), wo[...], preferred_element_type=F32)
        residual = (fr[...].reshape(NX * 2 * ROWS, D).astype(F32) + biased).astype(BF16)
        rs[...] = residual.reshape(NX, 2 * ROWS, D)
        residual_over.start()
        ffn_in = layer_norm(residual, ffg[...]).astype(BF16)
        hidden = gelu(jnp.dot(ffn_in, wu[...], preferred_element_type=F32)).astype(BF16)
        for h in (0, 1):
            part = jnp.dot(hidden, wd[:, h * half : (h + 1) * half], preferred_element_type=F32)
            yo[h] = part.astype(BF16).reshape(NX, 2 * ROWS, half)
            for copy in parts_out[h]:
                copy.start()
        for h in (0, 1):
            cols = slice(h * half, (h + 1) * half)
            done = rs[0, ROWS:, cols].astype(F32) + yo[h, 0, ROWS:, :].astype(F32)
            for e in (1, 3, 2):
                arrived(xr.at[h, e], r_xr.at[h, e])
                done = done + xr[h, e].astype(F32)
            out[:, cols] = done.astype(BF16)

    @pl.when(c == 0)
    def _():
        arrived(rc, r_rc)
        for h in (0, 1):
            cols = slice(h * half, (h + 1) * half)
            done = rc[:, cols].astype(F32)
            for e in (0, 1, 3, 2):
                arrived(xr.at[h, e], r_xr.at[h, e])
                done = done + xr[h, e].astype(F32)
            out[:, cols] = done.astype(BF16)

    finish()


def local(*args):
    dma = pltpu.SemaphoreType.DMA
    vm = pltpu.VMEM
    rows = 2 * ROWS
    return pl.pallas_call(
        kernel,
        out_shape=jax.ShapeDtypeStruct((ROWS, D), BF16),
        in_specs=[pl.BlockSpec(memory_space=pltpu.HBM)] * 10,
        out_specs=pl.BlockSpec(memory_space=pltpu.VMEM),
        scratch_shapes=[
            vm((NX, rows, D), BF16),
            vm((D,), F32),
            vm((D,), F32),
            vm((D, BIAS), BF16),
            vm((2, PH, BIAS), BF16),
            vm((2, PH, BIAS), BF16),
            vm((4, 256), jnp.int32),
            vm((BIAS, D), BF16),
            vm((D, FFL), BF16),
            vm((FFL, D), BF16),
            vm((rows, BIAS), BF16),
            vm((4, NY, 2 * rows, BIAS), BF16),
            vm((4, 3, 2 * rows, BIAS), BF16),
            vm((4, 2 * rows, BIAS), F32),
            vm((4, 3, 2 * rows, BIAS), BF16),
            vm((4, 2 * rows, BIAS), BF16),
            vm((16, rows, BIAS), BF16),
            vm((NY, 4, 1, 128), F32),
            vm((3, 4, 1, 128), F32),
            vm((4, 1, 128), F32),
            vm((16, 1, 128), F32),
            vm((NX, rows, BIAS), BF16),
            vm((NX, rows, D), BF16),
            vm((2, NX, rows, D // 2), BF16),
            vm((2, NX, ROWS, D // 2), BF16),
            vm((ROWS, D), BF16),
            vm((16, 128), F32),
            vm((STEP, 2 * PH), BF16),
            vm((rows, BIAS), BF16),
            dma((10,)),
            dma((2,)), dma((2,)),
            dma, dma,
            dma, dma,
            dma((10,)), dma((8,)), dma, dma((8,)),
            dma((4, 3)), dma((4, 3)),
            dma((4, 3)), dma((4, 3)),
            dma((8,)), dma((16,)),
            dma((3,)), dma((3,)),
            dma((8,)), dma,
            dma((3,)), dma((3,)),
            dma((3,)), dma((3,)),
            dma((2, 8)), dma((2, 4)),
            dma, dma,
        ],
        compiler_params=pltpu.CompilerParams(
            collective_id=0, has_side_effects=True, vmem_limit_bytes=56 * 2**20
        ),
        name="layer",
    )(*args)


def solution(mesh):
    placed = (
        P(("dp", "bank"), None),
        P(),
        P(),
        P("bank", None),
        P("bank", None),
        P(),
        P(),
        P(),
        P(None, "dp"),
        P("dp", None),
    )
    return jax.shard_map(
        local, mesh=mesh, in_specs=placed, out_specs=P(("dp", "bank"), None), check_vma=False
    )
```

```python
import jax
import jax.numpy as jnp
from jax import lax
from jax.experimental import pallas as pl
from jax.experimental.pallas import tpu as pltpu
from jax.sharding import PartitionSpec as P

MESH = pl.DeviceIdType.MESH
F32 = jnp.float32
BF16 = jnp.bfloat16
CAP = 30.0
LOG2E = 1.4426950408889634
NEAR = (0, 1, -1, 2, -2, 3, -3, 4)
FAR = (-4, 5, -5, 6, -6, 7, -7, 8)
NZ, NY, NX = 16, 4, 4
D, FFL, BIAS = 1280, 640, 256
ROWS = 16
PH = 1024
STEP = 256


def layer_norm(values, gain):
    wide = values.astype(F32)
    center = jnp.mean(wide, axis=-1, keepdims=True)
    moved = wide - center
    spread = jnp.mean(moved * moved, axis=-1, keepdims=True)
    return moved * lax.rsqrt(spread + 1e-05) * gain[None, :]


def gelu(v):
    return 0.5 * v * (1.0 + lax.erf(v * 0.7071067811865476))


def kernel(
    frames, ln_gain, w_query, keys, values, active, w_out, ffn_gain, w_up, w_down, out,
    fr, lng, ffg, wq, kb, vb, act, wo, wu, wd,
    qown, qb, pb, po, ry, zs, rz, ty, tr, ts, tz, cx, rs, yo, xr, rc, bias, wb, upper,
    ld, s_kv, r_kv, s_fr, r_fr, s_qx, r_qx, s_q, r_q, r_up, s_fw, s_yf, r_yf, s_ry, r_ry, s_rz, r_rz,
    s_ty, r_ty, s_tz, r_tz, s_xf, r_xf, s_xa, r_xa, s_xr, r_xr, s_rc, r_rc,
):
    x = lax.axis_index("dp")
    b = lax.axis_index("bank")
    c = lax.rem(b, 2)
    y = lax.rem(b // 2, NY)
    z = b // (2 * NY)

    def dev(dx=0, dz=0, dy=0, core=None):
        cz = lax.rem(z + dz + 2 * NZ, NZ)
        cy = lax.rem(y + dy + NY, NY)
        return (lax.rem(x + dx + NX, NX), (cz * NY + cy) * 2 + (c if core is None else core))

    sibling = dev(core=1 - c)

    def send(src, dst, ssem, rsem, to):
        return pltpu.make_async_remote_copy(
            src_ref=src, dst_ref=dst, send_sem=ssem, recv_sem=rsem, device_id=to, device_id_type=MESH
        )

    def arrived(dst, rsem):
        send(dst, dst, rsem, rsem, sibling).wait_recv()

    loads = [
        pltpu.make_async_copy(src, dst, ld.at[n])
        for n, (src, dst) in enumerate(
            (
                (frames, fr.at[0, pl.ds(ROWS, ROWS)]),
                (ln_gain, lng),
                (w_query, wq),
                (active, act),
                (keys, kb.at[c]),
                (values, vb.at[c]),
                (w_out, wo),
                (ffn_gain, ffg),
                (w_up, wu),
                (w_down, wd),
            )
        )
    ]
    for load in loads[:4]:
        load.start()

    sent, sent0, sent1 = [], [], []

    def finish():
        for copy in sent:
            copy.wait_send()

        @pl.when(c == 0)
        def _():
            for copy in sent0:
                copy.wait_send()

        @pl.when(c == 1)
        def _():
            for copy in sent1:
                copy.wait_send()

    barrier = pltpu.get_barrier_semaphore()

    def greet(to):
        pl.semaphore_signal(barrier, inc=1, device_id=to, device_id_type=MESH)

    @pl.when(c == 1)
    def _():
        greet(sibling)
        for dz in (4, -4, 3, -3, 2, -2, 1, -1):
            greet(dev(dz=dz))
        for e in (2, 1, 3):
            greet(dev(dy=e))
            greet(dev(dx=e))

    @pl.when(c == 0)
    def _():
        for dz in NEAR[::-1]:
            greet(dev(dz=dz, core=1))
        for e in (2, 1, 3):
            greet(dev(dy=e, core=1))
            greet(dev(dx=e, core=1))

    for n in range(4):
        loads[n].wait()
    for load in loads[4:]:
        load.start()
    normed = layer_norm(fr[0, ROWS:, :], lng[...]).astype(BF16)
    qown[pl.ds(ROWS, ROWS), :] = jnp.dot(normed, wq[...], preferred_element_type=F32).astype(BF16)

    first = (z * NY + y) * 16
    ids = first + lax.broadcasted_iota(jnp.int32, (16, 256), 0)
    hits = jnp.where(ids == act[pl.ds(x, 1), :], 1.0, 0.0).astype(F32)
    found = jnp.max(hits, axis=1, keepdims=True)
    ty[...] = jnp.zeros_like(ty)
    bias[...] = jnp.broadcast_to(jnp.where(found > 0.5, 0.0, -512.0).astype(F32), (16, 128))

    keys_over = send(keys, kb.at[c], s_kv.at[0], r_kv.at[0], sibling)
    values_over = send(values, vb.at[c], s_kv.at[1], r_kv.at[1], sibling)
    query_over = send(qown.at[pl.ds(ROWS, ROWS)], qown.at[pl.ds(0, ROWS)], s_qx, r_qx, sibling)
    frames_over = send(frames, fr.at[0, pl.ds(0, ROWS)], s_fr, r_fr, sibling)

    def slot(i):
        return qb.at[i // 2, 0, pl.ds((i % 2) * 2 * ROWS, 2 * ROWS)]

    query_out = [
        send(qown, upper, s_q.at[9], r_up, dev(dz=-4, core=1)),
        send(qown, slot(0), s_q.at[8], r_q.at[0], dev(dz=4, core=1)),
    ] + [
        send(qown, slot(i), s_q.at[i], r_q.at[i], dev(dz=-NEAR[i], core=0)) for i in range(7, -1, -1)
    ]
    relay_down = [
        send(upper, slot(2 * n - 1), s_fw.at[2 * n - 1], r_q.at[2 * n - 1], dev(dz=-n, core=1)) for n in (4, 3, 2, 1)
    ]
    relay_up = [send(slot(0), slot(2 * n), s_fw.at[2 * n], r_q.at[2 * n], dev(dz=n, core=1)) for n in (3, 2, 1)]

    def forward(k, e):
        return send(qb.at[k, 0], qb.at[k, NY - e], s_yf.at[k, e - 1], r_yf.at[k, NY - e - 1], dev(dy=e))

    sent0 += [query_over, frames_over]
    sent1 += query_out + relay_down + relay_up
    sent += [keys_over, values_over]

    @pl.when(c == 0)
    def _():
        pl.semaphore_wait(barrier, 1)
        query_over.start()

    @pl.when(c == 1)
    def _():
        pl.semaphore_wait(barrier, 28)
        arrived(qown.at[pl.ds(0, ROWS)], r_qx)
        for copy in query_out:
            copy.start()

    keys_over.start()
    values_over.start()

    @pl.when(c == 0)
    def _():
        frames_over.start()

    @pl.when(c == 1)
    def _():
        arrived(upper, r_up)
        for copy in relay_down:
            copy.start()

    arrived(slot(0), r_q.at[0])

    @pl.when(c == 1)
    def _():
        for copy in relay_up:
            copy.start()

    for k in range(4):
        for i in (2 * k, 2 * k + 1):
            if i:
                arrived(slot(i), r_q.at[i])
        for e in (2, 1, 3):
            forward(k, e).start()
    sent += [forward(k, e) for k in range(4) for e in (1, 2, 3)]

    frames_out = [send(fr.at[0], fr.at[NX - e], s_xf.at[e - 1], r_xf.at[NX - e - 1], dev(dx=e)) for e in (2, 1, 3)]
    sent1 += frames_out

    @pl.when(c == 1)
    def _():
        arrived(fr.at[0, pl.ds(0, ROWS)], r_fr)
        for copy in frames_out:
            copy.start()

    for n in range(4, 6):
        loads[n].wait()
    arrived(kb.at[1 - c], r_kv.at[0])
    arrived(vb.at[1 - c], r_kv.at[1])

    def give_back(k, e):
        return send(pb.at[k, e - 1], ry.at[k, NY - e - 1], s_ry.at[k, e - 1], r_ry.at[k, NY - e - 1], dev(dy=e))

    scale = 1.0 / (CAP * BIAS**0.5)

    def owner(i):
        return dev(dz=NEAR[i] + (FAR[i] - NEAR[i]) * c, core=1)

    def to_owner(k, j):
        i = 2 * k + j
        return send(
            zs.at[k, pl.ds(j * 2 * ROWS, 2 * ROWS)], rz.at[c * 8 + i], s_rz.at[i], r_rz.at[c * 8 + i], owner(i)
        )

    def add_up(k):
        total = po[k]
        for e in (1, 3, 2):
            arrived(ry.at[k, e - 1], r_ry.at[k, e - 1])
            total = total + ry[k, e - 1].astype(F32)
        zs[k] = total.astype(BF16)
        for j in (1, 0):
            to_owner(k, j).start()

    def attend(k, carry):
        pl.when((k == 3) & (c == 0))(lambda: add_up(0))
        for e in (1, 3, 2):
            arrived(qb.at[k, e], r_yf.at[k, e - 1])
        q = qb[k].reshape(STEP, BIAS)
        tot = jnp.zeros((STEP, 128), F32)
        for p in range(2 * PH // STEP):
            h, at = (p * STEP) // PH, (p * STEP) % PH
            raw = lax.dot_general(
                q, kb[h, pl.ds(at, STEP), :], (((1,), (1,)), ((), ())), preferred_element_type=F32
            )
            off = jnp.concatenate([bias[pl.ds(2 * p, 1), :], bias[pl.ds(2 * p + 1, 1), :]], axis=1)
            weight = jnp.exp2(jnp.tanh(raw * scale) * (CAP * LOG2E) + off)
            tot = tot + (weight[:, :128] + weight[:, 128:])
            wb[:, p * STEP : (p + 1) * STEP] = weight.astype(BF16)
        num = jnp.dot(wb[...], vb[...].reshape(2 * PH, BIAS), preferred_element_type=F32)
        part = 4 * ROWS
        po[k] = num[:part]
        for e in (2, 1, 3):
            pb[k, e - 1] = num[e * part : (e + 1) * part].astype(BF16)
            give_back(k, e).start()
        row = lax.dot_general(
            jnp.ones((8, 128), BF16), tot.astype(BF16), (((1,), (1,)), ((), ())), preferred_element_type=F32
        )
        for e in range(NY):
            ty[e, k, :, :part] = row[:1, e * part : (e + 1) * part]
        return carry

    lax.fori_loop(0, 4, attend, 0)
    sent += [give_back(k, e) for k in range(4) for e in (1, 2, 3)]

    totals_back = [send(ty.at[e], tr.at[NY - e - 1], s_ty.at[e - 1], r_ty.at[NY - e - 1], dev(dy=e)) for e in (2, 1, 3)]
    for copy in totals_back:
        copy.start()
    sent += totals_back

    pl.when(c == 1)(lambda: add_up(0))
    for k in range(1, 4):
        add_up(k)
    totals = ty[0]
    for e in (1, 3, 2):
        arrived(tr.at[e - 1], r_ty.at[e - 1])
        totals = totals + tr[e - 1]
    ts[...] = totals
    totals_out = [
        send(ts.at[i // 2], tz.at[c * 8 + i], s_tz.at[i], r_tz, owner(i))
        for i in range(7, -1, -1)
    ]
    for copy in totals_out:
        copy.start()
    sent += totals_out
    sent += [to_owner(k, j) for k in range(4) for j in (0, 1)]

    for n in range(6, 10):
        loads[n].wait()

    half = D // 2
    context_out = [send(cx.at[0], cx.at[NX - e], s_xa.at[e - 1], r_xa.at[NX - e - 1], dev(dx=e)) for e in (2, 1, 3)]
    residual_over = send(rs.at[0, pl.ds(0, ROWS)], rc, s_rc, r_rc, sibling)
    parts_out = [
        [
            send(
                yo.at[h, e, pl.ds(core * ROWS, ROWS)],
                xr.at[h, (NX - e) % NX],
                s_xr.at[h, e * 2 + core],
                r_xr.at[h, (NX - e) % NX],
                dev(dx=e, core=core),
            )
            for e, core in ((2, 0), (2, 1), (1, 0), (1, 1), (3, 0), (3, 1), (0, 0))
        ]
        for h in (0, 1)
    ]
    sent1 += context_out + parts_out[0] + parts_out[1] + [residual_over]

    @pl.when(c == 1)
    def _():
        for e in (1, 3, 2):
            arrived(fr.at[e], r_xf.at[e - 1])
        total = jnp.zeros((2 * ROWS, BIAS), F32)
        for n in range(16):
            arrived(rz.at[n], r_rz.at[n])
            total = total + rz[n].astype(F32)
        arrived(tz, r_tz)
        even, odd = tz[0], tz[1]
        for n in range(2, 16, 2):
            even, odd = even + tz[n], odd + tz[n + 1]
        gap = lax.broadcasted_iota(jnp.int32, (2 * ROWS, 128), 1) - lax.broadcasted_iota(jnp.int32, (2 * ROWS, 128), 0)
        spread = jnp.where(gap == 0, even, 0.0) + jnp.where(gap == 2 * ROWS, odd, 0.0)
        context = total / jnp.sum(spread, axis=1, keepdims=True)
        power = jnp.mean(context * context, axis=1, keepdims=True)
        cx[0] = (context * lax.rsqrt(power + 0.0001)).astype(BF16)
        for copy in context_out:
            copy.start()
        for e in (1, 3, 2):
            arrived(cx.at[e], r_xa.at[e - 1])
        biased = jnp.dot(cx[...].reshape(NX * 2 * ROWS, BIAS), wo[...], preferred_element_type=F32)
        residual = (fr[...].reshape(NX * 2 * ROWS, D).astype(F32) + biased).astype(BF16)
        rs[...] = residual.reshape(NX, 2 * ROWS, D)
        residual_over.start()
        ffn_in = layer_norm(residual, ffg[...]).astype(BF16)
        hidden = gelu(jnp.dot(ffn_in, wu[...], preferred_element_type=F32)).astype(BF16)
        for h in (0, 1):
            part = jnp.dot(hidden, wd[:, h * half : (h + 1) * half], preferred_element_type=F32)
            yo[h] = part.astype(BF16).reshape(NX, 2 * ROWS, half)
            for copy in parts_out[h]:
                copy.start()
        for h in (0, 1):
            cols = slice(h * half, (h + 1) * half)
            done = rs[0, ROWS:, cols].astype(F32) + yo[h, 0, ROWS:, :].astype(F32)
            for e in (1, 3, 2):
                arrived(xr.at[h, e], r_xr.at[h, e])
                done = done + xr[h, e].astype(F32)
            out[:, cols] = done.astype(BF16)

    @pl.when(c == 0)
    def _():
        arrived(rc, r_rc)
        for h in (0, 1):
            cols = slice(h * half, (h + 1) * half)
            done = rc[:, cols].astype(F32)
            for e in (0, 1, 3, 2):
                arrived(xr.at[h, e], r_xr.at[h, e])
                done = done + xr[h, e].astype(F32)
            out[:, cols] = done.astype(BF16)

    finish()


def local(*args):
    dma = pltpu.SemaphoreType.DMA
    vm = pltpu.VMEM
    rows = 2 * ROWS
    return pl.pallas_call(
        kernel,
        out_shape=jax.ShapeDtypeStruct((ROWS, D), BF16),
        in_specs=[pl.BlockSpec(memory_space=pltpu.HBM)] * 10,
        out_specs=pl.BlockSpec(memory_space=pltpu.VMEM),
        scratch_shapes=[
            vm((NX, rows, D), BF16),
            vm((D,), F32),
            vm((D,), F32),
            vm((D, BIAS), BF16),
            vm((2, PH, BIAS), BF16),
            vm((2, PH, BIAS), BF16),
            vm((4, 256), jnp.int32),
            vm((BIAS, D), BF16),
            vm((D, FFL), BF16),
            vm((FFL, D), BF16),
            vm((rows, BIAS), BF16),
            vm((4, NY, 2 * rows, BIAS), BF16),
            vm((4, 3, 2 * rows, BIAS), BF16),
            vm((4, 2 * rows, BIAS), F32),
            vm((4, 3, 2 * rows, BIAS), BF16),
            vm((4, 2 * rows, BIAS), BF16),
            vm((16, rows, BIAS), BF16),
            vm((NY, 4, 1, 128), F32),
            vm((3, 4, 1, 128), F32),
            vm((4, 1, 128), F32),
            vm((16, 1, 128), F32),
            vm((NX, rows, BIAS), BF16),
            vm((NX, rows, D), BF16),
            vm((2, NX, rows, D // 2), BF16),
            vm((2, NX, ROWS, D // 2), BF16),
            vm((ROWS, D), BF16),
            vm((16, 128), F32),
            vm((STEP, 2 * PH), BF16),
            vm((rows, BIAS), BF16),
            dma((10,)),
            dma((2,)), dma((2,)),
            dma, dma,
            dma, dma,
            dma((10,)), dma((8,)), dma, dma((8,)),
            dma((4, 3)), dma((4, 3)),
            dma((4, 3)), dma((4, 3)),
            dma((8,)), dma((16,)),
            dma((3,)), dma((3,)),
            dma((8,)), dma,
            dma((3,)), dma((3,)),
            dma((3,)), dma((3,)),
            dma((2, 8)), dma((2, 4)),
            dma, dma,
        ],
        compiler_params=pltpu.CompilerParams(
            collective_id=0, has_side_effects=True, vmem_limit_bytes=56 * 2**20
        ),
        name="layer",
    )(*args)


def solution(mesh):
    placed = (
        P(("dp", "bank"), None),
        P(),
        P(),
        P("bank", None),
        P("bank", None),
        P(),
        P(),
        P(),
        P(None, "dp"),
        P("dp", None),
    )
    return jax.shard_map(
        local, mesh=mesh, in_specs=placed, out_specs=P(("dp", "bank"), None), check_vma=False
    )
```

```python
import jax
import jax.numpy as jnp
from jax import lax
from jax.experimental import pallas as pl
from jax.experimental.pallas import tpu as pltpu
from jax.sharding import PartitionSpec as P

MESH = pl.DeviceIdType.MESH
F32 = jnp.float32
BF16 = jnp.bfloat16
CAP = 30.0
LOG2E = 1.4426950408889634
NEAR = (0, 1, -1, 2, -2, 3, -3, 4)
FAR = (-4, 5, -5, 6, -6, 7, -7, 8)
NZ, NY, NX = 16, 4, 4
D, FFL, BIAS = 1280, 640, 256
ROWS = 16
PH = 1024
STEP = 256


def layer_norm(values, gain):
    wide = values.astype(F32)
    center = jnp.mean(wide, axis=-1, keepdims=True)
    moved = wide - center
    spread = jnp.mean(moved * moved, axis=-1, keepdims=True)
    return moved * lax.rsqrt(spread + 1e-05) * gain[None, :]


def gelu(v):
    return 0.5 * v * (1.0 + lax.erf(v * 0.7071067811865476))


def kernel(
    frames, ln_gain, w_query, keys, values, active, w_out, ffn_gain, w_up, w_down, out,
    fr, lng, ffg, wq, kb, vb, act, wo, wu, wd,
    qown, qb, pb, po, ry, zs, rz, ty, tr, ts, tz, cx, rs, yo, xr, rc, bias, wb, upper,
    ld, s_kv, r_kv, s_fr, r_fr, s_q, r_q, r_up, s_fw, s_yf, r_yf, s_ry, r_ry, s_rz, r_rz,
    s_ty, r_ty, s_tz, r_tz, s_xf, r_xf, s_xa, r_xa, s_xr, r_xr, s_rc, r_rc,
):
    x = lax.axis_index("dp")
    b = lax.axis_index("bank")
    c = lax.rem(b, 2)
    y = lax.rem(b // 2, NY)
    z = b // (2 * NY)

    def dev(dx=0, dz=0, dy=0, core=None):
        cz = lax.rem(z + dz + 2 * NZ, NZ)
        cy = lax.rem(y + dy + NY, NY)
        return (lax.rem(x + dx + NX, NX), (cz * NY + cy) * 2 + (c if core is None else core))

    sibling = dev(core=1 - c)

    def send(src, dst, ssem, rsem, to):
        return pltpu.make_async_remote_copy(
            src_ref=src, dst_ref=dst, send_sem=ssem, recv_sem=rsem, device_id=to, device_id_type=MESH
        )

    def arrived(dst, rsem):
        send(dst, dst, rsem, rsem, sibling).wait_recv()

    loads = [
        pltpu.make_async_copy(src, dst, ld.at[n])
        for n, (src, dst) in enumerate(
            (
                (frames, fr.at[0, pl.ds(ROWS, ROWS)]),
                (ln_gain, lng),
                (w_query, wq),
                (active, act),
                (keys, kb.at[c]),
                (values, vb.at[c]),
                (w_out, wo),
                (ffn_gain, ffg),
                (w_up, wu),
                (w_down, wd),
            )
        )
    ]
    for load in loads[:4]:
        load.start()

    sent, sent0, sent1 = [], [], []

    def finish():
        for copy in sent:
            copy.wait_send()

        @pl.when(c == 0)
        def _():
            for copy in sent0:
                copy.wait_send()

        @pl.when(c == 1)
        def _():
            for copy in sent1:
                copy.wait_send()

    barrier = pltpu.get_barrier_semaphore()

    def greet(to):
        pl.semaphore_signal(barrier, inc=1, device_id=to, device_id_type=MESH)

    @pl.when(c == 1)
    def _():
        greet(sibling)
        for dz in (4, -4, 3, -3, 2, -2, 1, -1):
            greet(dev(dz=dz))
        for e in (2, 1, 3):
            greet(dev(dy=e))
            greet(dev(dx=e))

    @pl.when(c == 0)
    def _():
        for dz in NEAR[::-1]:
            greet(dev(dz=dz, core=1))
        for e in (2, 1, 3):
            greet(dev(dy=e, core=1))
            greet(dev(dx=e, core=1))

    keys_over = send(keys, kb.at[c], s_kv.at[0], r_kv.at[0], sibling)
    values_over = send(values, vb.at[c], s_kv.at[1], r_kv.at[1], sibling)
    frames_over = send(frames, fr.at[0, pl.ds(0, ROWS)], s_fr, r_fr, sibling)

    def slot(i):
        return qb.at[i // 2, 0, pl.ds((i % 2) * 2 * ROWS, 2 * ROWS)]

    query_out = [
        send(qown, upper, s_q.at[9], r_up, dev(dz=-4, core=1)),
        send(qown, slot(0), s_q.at[8], r_q.at[0], dev(dz=4, core=1)),
    ] + [
        send(qown, slot(i), s_q.at[i], r_q.at[i], dev(dz=-NEAR[i], core=0)) for i in range(7, -1, -1)
    ]
    relay_down = [
        send(upper, slot(2 * n - 1), s_fw.at[2 * n - 1], r_q.at[2 * n - 1], dev(dz=-n, core=1)) for n in (4, 3, 2, 1)
    ]
    relay_up = [send(slot(0), slot(2 * n), s_fw.at[2 * n], r_q.at[2 * n], dev(dz=n, core=1)) for n in (3, 2, 1)]

    def forward(k, e):
        return send(qb.at[k, 0], qb.at[k, NY - e], s_yf.at[k, e - 1], r_yf.at[k, NY - e - 1], dev(dy=e))

    sent0 += [frames_over]
    sent1 += query_out + relay_down + relay_up
    sent += [keys_over, values_over]

    @pl.when(c == 0)
    def _():
        pl.semaphore_wait(barrier, 1)
        frames_over.start()
        for load in loads[4:]:
            load.start()
        for load in loads[:3]:
            load.wait()

    @pl.when(c == 1)
    def _():
        loads[0].wait()
        loads[1].wait()
        arrived(fr.at[0, pl.ds(0, ROWS)], r_fr)
        normed = layer_norm(fr[0], lng[...]).astype(BF16)
        loads[2].wait()
        qown[...] = jnp.dot(normed, wq[...], preferred_element_type=F32).astype(BF16)
        for load in loads[4:]:
            load.start()
        pl.semaphore_wait(barrier, 28)
        for copy in query_out:
            copy.start()

    keys_over.start()
    values_over.start()

    loads[3].wait()
    first = (z * NY + y) * 16
    ids = first + lax.broadcasted_iota(jnp.int32, (16, 256), 0)
    hits = jnp.where(ids == act[pl.ds(x, 1), :], 1.0, 0.0).astype(F32)
    found = jnp.max(hits, axis=1, keepdims=True)
    bias[...] = jnp.broadcast_to(jnp.where(found > 0.5, 0.0, -512.0).astype(F32), (16, 128))
    ty[...] = jnp.zeros_like(ty)

    @pl.when(c == 1)
    def _():
        arrived(upper, r_up)
        for copy in relay_down:
            copy.start()

    arrived(slot(0), r_q.at[0])

    @pl.when(c == 1)
    def _():
        for copy in relay_up:
            copy.start()

    for k in range(4):
        for i in (2 * k, 2 * k + 1):
            if i:
                arrived(slot(i), r_q.at[i])
        for e in (2, 1, 3):
            forward(k, e).start()
    sent += [forward(k, e) for k in range(4) for e in (1, 2, 3)]

    frames_out = [send(fr.at[0], fr.at[NX - e], s_xf.at[e - 1], r_xf.at[NX - e - 1], dev(dx=e)) for e in (2, 1, 3)]
    sent1 += frames_out

    @pl.when(c == 1)
    def _():
        for copy in frames_out:
            copy.start()

    for n in range(4, 6):
        loads[n].wait()
    arrived(kb.at[1 - c], r_kv.at[0])
    arrived(vb.at[1 - c], r_kv.at[1])

    def give_back(k, e):
        return send(pb.at[k, e - 1], ry.at[k, NY - e - 1], s_ry.at[k, e - 1], r_ry.at[k, NY - e - 1], dev(dy=e))

    scale = 1.0 / (CAP * BIAS**0.5)

    def owner(i):
        return dev(dz=NEAR[i] + (FAR[i] - NEAR[i]) * c, core=1)

    def to_owner(k, j):
        i = 2 * k + j
        return send(
            zs.at[k, pl.ds(j * 2 * ROWS, 2 * ROWS)], rz.at[c * 8 + i], s_rz.at[i], r_rz.at[c * 8 + i], owner(i)
        )

    def add_up(k):
        total = po[k]
        for e in (1, 3, 2):
            arrived(ry.at[k, e - 1], r_ry.at[k, e - 1])
            total = total + ry[k, e - 1].astype(F32)
        zs[k] = total.astype(BF16)
        for j in (1, 0):
            to_owner(k, j).start()

    spans = (pl.ds(0, 3), pl.ds(3, 1))
    totals_back = [
        [
            send(ty.at[e, span], tr.at[NY - e - 1, span], s_ty.at[n, e - 1], r_ty.at[n, NY - e - 1], dev(dy=e))
            for e in (2, 1, 3)
        ]
        for n, span in enumerate(spans)
    ]
    totals_out = [
        send(ts.at[i // 2], tz.at[c * 8 + i], s_tz.at[i], r_tz, owner(i)) for i in range(8)
    ]

    def add_totals(n):
        span = spans[n]
        totals = ty[0, span]
        for e in (1, 3, 2):
            arrived(tr.at[e - 1, span], r_ty.at[n, e - 1])
            totals = totals + tr[e - 1, span]
        ts[span] = totals
        for copy in totals_out[6:] if n else totals_out[:6]:
            copy.start()

    def attend(k, carry):
        pl.when((k == 3) & (c == 0))(lambda: add_up(0))
        for e in (1, 3, 2):
            arrived(qb.at[k, e], r_yf.at[k, e - 1])
        q = qb[k].reshape(STEP, BIAS)
        tot = jnp.zeros((STEP, 128), F32)
        for p in range(2 * PH // STEP):
            h, at = (p * STEP) // PH, (p * STEP) % PH
            raw = lax.dot_general(
                q, kb[h, pl.ds(at, STEP), :], (((1,), (1,)), ((), ())), preferred_element_type=F32
            )
            off = jnp.concatenate([bias[pl.ds(2 * p, 1), :], bias[pl.ds(2 * p + 1, 1), :]], axis=1)
            weight = jnp.exp2(jnp.tanh(raw * scale) * (CAP * LOG2E) + off)
            tot = tot + (weight[:, :128] + weight[:, 128:])
            wb[:, p * STEP : (p + 1) * STEP] = weight.astype(BF16)
        num = jnp.dot(wb[...], vb[...].reshape(2 * PH, BIAS), preferred_element_type=F32)
        part = 4 * ROWS
        po[k] = num[:part]
        for e in (2, 1, 3):
            pb[k, e - 1] = num[e * part : (e + 1) * part].astype(BF16)
            give_back(k, e).start()
        row = lax.dot_general(
            jnp.ones((8, 128), BF16), tot.astype(BF16), (((1,), (1,)), ((), ())), preferred_element_type=F32
        )
        for e in range(NY):
            ty[e, k, :, :part] = row[:1, e * part : (e + 1) * part]

        @pl.when(k == 2)
        def _():
            for copy in totals_back[0]:
                copy.start()

        return carry

    lax.fori_loop(0, 4, attend, 0)
    sent += [give_back(k, e) for k in range(4) for e in (1, 2, 3)]

    for copy in totals_back[1]:
        copy.start()
    sent += totals_back[0] + totals_back[1]

    pl.when(c == 1)(lambda: add_up(0))
    add_up(1)
    add_up(2)
    add_totals(0)
    add_up(3)
    add_totals(1)
    sent += totals_out
    sent += [to_owner(k, j) for k in range(4) for j in (0, 1)]

    for n in range(6, 10):
        loads[n].wait()

    half = D // 2
    context_out = [send(cx.at[0], cx.at[NX - e], s_xa.at[e - 1], r_xa.at[NX - e - 1], dev(dx=e)) for e in (2, 1, 3)]
    residual_over = send(rs.at[0, pl.ds(0, ROWS)], rc, s_rc, r_rc, sibling)
    parts_out = [
        [
            send(
                yo.at[h, e, pl.ds(core * ROWS, ROWS)],
                xr.at[h, (NX - e) % NX],
                s_xr.at[h, e * 2 + core],
                r_xr.at[h, (NX - e) % NX],
                dev(dx=e, core=core),
            )
            for e, core in ((2, 0), (2, 1), (1, 0), (1, 1), (3, 0), (3, 1), (0, 0))
        ]
        for h in (0, 1)
    ]
    sent1 += context_out + parts_out[0] + parts_out[1] + [residual_over]

    @pl.when(c == 1)
    def _():
        for e in (1, 3, 2):
            arrived(fr.at[e], r_xf.at[e - 1])
        total = jnp.zeros((2 * ROWS, BIAS), F32)
        for n in range(16):
            arrived(rz.at[n], r_rz.at[n])
            total = total + rz[n].astype(F32)
        arrived(tz, r_tz)
        even, odd = tz[0], tz[1]
        for n in range(2, 16, 2):
            even, odd = even + tz[n], odd + tz[n + 1]
        gap = lax.broadcasted_iota(jnp.int32, (2 * ROWS, 128), 1) - lax.broadcasted_iota(jnp.int32, (2 * ROWS, 128), 0)
        spread = jnp.where(gap == 0, even, 0.0) + jnp.where(gap == 2 * ROWS, odd, 0.0)
        context = total / jnp.sum(spread, axis=1, keepdims=True)
        power = jnp.mean(context * context, axis=1, keepdims=True)
        cx[0] = (context * lax.rsqrt(power + 0.0001)).astype(BF16)
        for copy in context_out:
            copy.start()
        for e in (1, 3, 2):
            arrived(cx.at[e], r_xa.at[e - 1])
        biased = jnp.dot(cx[...].reshape(NX * 2 * ROWS, BIAS), wo[...], preferred_element_type=F32)
        residual = (fr[...].reshape(NX * 2 * ROWS, D).astype(F32) + biased).astype(BF16)
        rs[...] = residual.reshape(NX, 2 * ROWS, D)
        residual_over.start()
        ffn_in = layer_norm(residual, ffg[...]).astype(BF16)
        hidden = gelu(jnp.dot(ffn_in, wu[...], preferred_element_type=F32)).astype(BF16)
        for h in (0, 1):
            part = jnp.dot(hidden, wd[:, h * half : (h + 1) * half], preferred_element_type=F32)
            yo[h] = part.astype(BF16).reshape(NX, 2 * ROWS, half)
            for copy in parts_out[h]:
                copy.start()
        for h in (0, 1):
            cols = slice(h * half, (h + 1) * half)
            done = rs[0, ROWS:, cols].astype(F32) + yo[h, 0, ROWS:, :].astype(F32)
            for e in (1, 3, 2):
                arrived(xr.at[h, e], r_xr.at[h, e])
                done = done + xr[h, e].astype(F32)
            out[:, cols] = done.astype(BF16)

    @pl.when(c == 0)
    def _():
        arrived(rc, r_rc)
        for h in (0, 1):
            cols = slice(h * half, (h + 1) * half)
            done = rc[:, cols].astype(F32)
            for e in (0, 1, 3, 2):
                arrived(xr.at[h, e], r_xr.at[h, e])
                done = done + xr[h, e].astype(F32)
            out[:, cols] = done.astype(BF16)

    finish()


def local(*args):
    dma = pltpu.SemaphoreType.DMA
    vm = pltpu.VMEM
    rows = 2 * ROWS
    return pl.pallas_call(
        kernel,
        out_shape=jax.ShapeDtypeStruct((ROWS, D), BF16),
        in_specs=[pl.BlockSpec(memory_space=pltpu.HBM)] * 10,
        out_specs=pl.BlockSpec(memory_space=pltpu.VMEM),
        scratch_shapes=[
            vm((NX, rows, D), BF16),
            vm((D,), F32),
            vm((D,), F32),
            vm((D, BIAS), BF16),
            vm((2, PH, BIAS), BF16),
            vm((2, PH, BIAS), BF16),
            vm((4, 256), jnp.int32),
            vm((BIAS, D), BF16),
            vm((D, FFL), BF16),
            vm((FFL, D), BF16),
            vm((rows, BIAS), BF16),
            vm((4, NY, 2 * rows, BIAS), BF16),
            vm((4, 3, 2 * rows, BIAS), BF16),
            vm((4, 2 * rows, BIAS), F32),
            vm((4, 3, 2 * rows, BIAS), BF16),
            vm((4, 2 * rows, BIAS), BF16),
            vm((16, rows, BIAS), BF16),
            vm((NY, 4, 1, 128), F32),
            vm((3, 4, 1, 128), F32),
            vm((4, 1, 128), F32),
            vm((16, 1, 128), F32),
            vm((NX, rows, BIAS), BF16),
            vm((NX, rows, D), BF16),
            vm((2, NX, rows, D // 2), BF16),
            vm((2, NX, ROWS, D // 2), BF16),
            vm((ROWS, D), BF16),
            vm((16, 128), F32),
            vm((STEP, 2 * PH), BF16),
            vm((rows, BIAS), BF16),
            dma((10,)),
            dma((2,)), dma((2,)),
            dma, dma,
            dma((10,)), dma((8,)), dma, dma((8,)),
            dma((4, 3)), dma((4, 3)),
            dma((4, 3)), dma((4, 3)),
            dma((8,)), dma((16,)),
            dma((2, 3)), dma((2, 3)),
            dma((8,)), dma,
            dma((3,)), dma((3,)),
            dma((3,)), dma((3,)),
            dma((2, 8)), dma((2, 4)),
            dma, dma,
        ],
        compiler_params=pltpu.CompilerParams(
            collective_id=0, has_side_effects=True, vmem_limit_bytes=56 * 2**20
        ),
        name="layer",
    )(*args)


def solution(mesh):
    placed = (
        P(("dp", "bank"), None),
        P(),
        P(),
        P("bank", None),
        P("bank", None),
        P(),
        P(),
        P(),
        P(None, "dp"),
        P("dp", None),
    )
    return jax.shard_map(
        local, mesh=mesh, in_specs=placed, out_specs=P(("dp", "bank"), None), check_vma=False
    )
```

```python
import jax
import jax.numpy as jnp
from jax import lax
from jax.experimental import pallas as pl
from jax.experimental.pallas import tpu as pltpu
from jax.sharding import PartitionSpec as P

MESH = pl.DeviceIdType.MESH
F32 = jnp.float32
BF16 = jnp.bfloat16
CAP = 30.0
LOG2E = 1.4426950408889634
NEAR = (0, 1, -1, 2, -2, 3, -3, 4)
FAR = (-4, 5, -5, 6, -6, 7, -7, 8)
NZ, NY, NX = 16, 4, 4
D, FFL, BIAS = 1280, 640, 256
ROWS = 16
PH = 1024
STEP = 256


def layer_norm(values, gain):
    wide = values.astype(F32)
    center = jnp.mean(wide, axis=-1, keepdims=True)
    moved = wide - center
    spread = jnp.mean(moved * moved, axis=-1, keepdims=True)
    return moved * lax.rsqrt(spread + 1e-05) * gain[None, :]


def gelu(v):
    return 0.5 * v * (1.0 + lax.erf(v * 0.7071067811865476))


def kernel(
    frames, ln_gain, w_query, keys, values, active, w_out, ffn_gain, w_up, w_down, out,
    fr, lng, ffg, wq, kb, vb, act, wo, wu, wd,
    qown, qb, pb, po, ry, zs, rz, ty, tr, ts, tz, cx, rs, yo, xr, rc, bias, wb, upper,
    ld, s_kv, r_kv, s_fr, r_fr, s_q, r_q, r_up, s_fw, s_yf, r_yf, s_ry, r_ry, s_rz, r_rz,
    s_ty, r_ty, s_tz, r_tz, s_xf, r_xf, s_xa, r_xa, s_xr, r_xr, s_rc, r_rc, turn,
):
    x = lax.axis_index("dp")
    b = lax.axis_index("bank")
    c = lax.rem(b, 2)
    y = lax.rem(b // 2, NY)
    z = b // (2 * NY)

    def dev(dx=0, dz=0, dy=0, core=None):
        cz = lax.rem(z + dz + 2 * NZ, NZ)
        cy = lax.rem(y + dy + NY, NY)
        return (lax.rem(x + dx + NX, NX), (cz * NY + cy) * 2 + (c if core is None else core))

    sibling = dev(core=1 - c)

    def send(src, dst, ssem, rsem, to):
        return pltpu.make_async_remote_copy(
            src_ref=src, dst_ref=dst, send_sem=ssem, recv_sem=rsem, device_id=to, device_id_type=MESH
        )

    def arrived(dst, rsem):
        send(dst, dst, rsem, rsem, sibling).wait_recv()

    loads = [
        pltpu.make_async_copy(src, dst, ld.at[n])
        for n, (src, dst) in enumerate(
            (
                (frames, fr.at[0, pl.ds(ROWS, ROWS)]),
                (ln_gain, lng),
                (w_query, wq),
                (active, act),
                (keys, kb.at[c]),
                (values, vb.at[c]),
                (w_out, wo),
                (ffn_gain, ffg),
                (w_up, wu),
                (w_down, wd),
            )
        )
    ]
    for load in loads[:4]:
        load.start()

    sent, sent0, sent1 = [], [], []

    def finish():
        for copy in sent:
            copy.wait_send()

        @pl.when(c == 0)
        def _():
            for copy in sent0:
                copy.wait_send()

        @pl.when(c == 1)
        def _():
            for copy in sent1:
                copy.wait_send()

    barrier = pltpu.get_barrier_semaphore()

    def greet(to):
        pl.semaphore_signal(barrier, inc=1, device_id=to, device_id_type=MESH)

    @pl.when(c == 1)
    def _():
        greet(sibling)
        for dz in (4, -4, 3, -3, 2, -2, 1, -1):
            greet(dev(dz=dz))
        for e in (2, 1, 3):
            greet(dev(dy=e))
            greet(dev(dx=e))

    @pl.when(c == 0)
    def _():
        for dz in NEAR[::-1]:
            greet(dev(dz=dz, core=1))
        for e in (2, 1, 3):
            greet(dev(dy=e, core=1))
            greet(dev(dx=e, core=1))

    keys_over = send(keys, kb.at[c], s_kv.at[0], r_kv.at[0], sibling)
    values_over = send(values, vb.at[c], s_kv.at[1], r_kv.at[1], sibling)
    frames_over = send(frames, fr.at[0, pl.ds(0, ROWS)], s_fr, r_fr, sibling)

    def slot(i):
        return qb.at[i // 2, 0, pl.ds((i % 2) * 2 * ROWS, 2 * ROWS)]

    query_out = [
        send(qown, upper, s_q.at[9], r_up, dev(dz=-4, core=1)),
        send(qown, slot(0), s_q.at[8], r_q.at[0], dev(dz=4, core=1)),
    ] + [
        send(qown, slot(i), s_q.at[i], r_q.at[i], dev(dz=-NEAR[i], core=0)) for i in range(7, -1, -1)
    ]
    relay_down = [
        send(upper, slot(2 * n - 1), s_fw.at[2 * n - 1], r_q.at[2 * n - 1], dev(dz=-n, core=1)) for n in (4, 3, 2, 1)
    ]
    relay_up = [send(slot(0), slot(2 * n), s_fw.at[2 * n], r_q.at[2 * n], dev(dz=n, core=1)) for n in (3, 2, 1)]

    def forward(k, e):
        return send(qb.at[k, 0], qb.at[k, NY - e], s_yf.at[k, e - 1], r_yf.at[k, NY - e - 1], dev(dy=e))

    sent0 += [frames_over]
    sent1 += query_out + relay_down + relay_up
    sent += [keys_over, values_over]

    @pl.when(c == 0)
    def _():
        pl.semaphore_wait(barrier, 1)
        frames_over.start()
        for load in loads[4:]:
            load.start()
        for load in loads[:3]:
            load.wait()

    @pl.when(c == 1)
    def _():
        loads[0].wait()
        loads[1].wait()
        arrived(fr.at[0, pl.ds(0, ROWS)], r_fr)
        normed = layer_norm(fr[0], lng[...]).astype(BF16)
        loads[2].wait()
        qown[...] = jnp.dot(normed, wq[...], preferred_element_type=F32).astype(BF16)
        for load in loads[4:]:
            load.start()
        pl.semaphore_wait(barrier, 28)
        for copy in query_out:
            copy.start()

    keys_over.start()
    values_over.start()

    loads[3].wait()
    first = (z * NY + y) * 16
    ids = first + lax.broadcasted_iota(jnp.int32, (16, 256), 0)
    hits = jnp.where(ids == act[pl.ds(x, 1), :], 1.0, 0.0).astype(F32)
    found = jnp.max(hits, axis=1, keepdims=True)
    bias[...] = jnp.broadcast_to(jnp.where(found > 0.5, 0.0, -512.0).astype(F32), (16, 128))
    ty[...] = jnp.zeros_like(ty)

    @pl.when(c == 1)
    def _():
        arrived(upper, r_up)
        for copy in relay_down:
            copy.start()

    arrived(slot(0), r_q.at[0])

    @pl.when(c == 1)
    def _():
        for copy in relay_up:
            copy.start()

    for k in range(4):
        for i in (2 * k, 2 * k + 1):
            if i:
                arrived(slot(i), r_q.at[i])
        for e in (2, 1, 3):
            forward(k, e).start()
    sent += [forward(k, e) for k in range(4) for e in (1, 2, 3)]

    for n in range(4, 6):
        loads[n].wait()
    arrived(kb.at[1 - c], r_kv.at[0])
    arrived(vb.at[1 - c], r_kv.at[1])

    def give_back(k, e):
        return send(pb.at[k, e - 1], ry.at[k, NY - e - 1], s_ry.at[k, e - 1], r_ry.at[k, NY - e - 1], dev(dy=e))

    scale = 1.0 / (CAP * BIAS**0.5)

    def owner(i):
        return dev(dz=NEAR[i] + (FAR[i] - NEAR[i]) * c, core=1)

    def to_owner(k, j):
        i = 2 * k + j
        return send(
            zs.at[k, pl.ds(j * 2 * ROWS, 2 * ROWS)], rz.at[c * 8 + i], s_rz.at[i], r_rz.at[c * 8 + i], owner(i)
        )

    def add_up(k):
        total = po[k]
        for e in (1, 3, 2):
            arrived(ry.at[k, e - 1], r_ry.at[k, e - 1])
            total = total + ry[k, e - 1].astype(F32)
        zs[k] = total.astype(BF16)
        for j in (1, 0):
            to_owner(k, j).start()

    spans = (pl.ds(0, 3), pl.ds(3, 1))
    totals_back = [
        [
            send(ty.at[e, span], tr.at[NY - e - 1, span], s_ty.at[n, e - 1], r_ty.at[n, NY - e - 1], dev(dy=e))
            for e in (2, 1, 3)
        ]
        for n, span in enumerate(spans)
    ]
    totals_out = [
        send(ts.at[i // 2], tz.at[c * 8 + i], s_tz.at[i], r_tz, owner(i)) for i in range(8)
    ]

    def add_totals(n):
        span = spans[n]
        totals = ty[0, span]
        for e in (1, 3, 2):
            arrived(tr.at[e - 1, span], r_ty.at[n, e - 1])
            totals = totals + tr[e - 1, span]
        ts[span] = totals
        for copy in totals_out[6:] if n else totals_out[:6]:
            copy.start()

    def attend(k, carry):
        for e in (1, 3, 2):
            arrived(qb.at[k, e], r_yf.at[k, e - 1])
        q = qb[k].reshape(STEP, BIAS)
        tot = jnp.zeros((STEP, 128), F32)
        for p in range(2 * PH // STEP):
            h, at = (p * STEP) // PH, (p * STEP) % PH
            raw = lax.dot_general(
                q, kb[h, pl.ds(at, STEP), :], (((1,), (1,)), ((), ())), preferred_element_type=F32
            )
            off = jnp.concatenate([bias[pl.ds(2 * p, 1), :], bias[pl.ds(2 * p + 1, 1), :]], axis=1)
            weight = jnp.exp2(jnp.tanh(raw * scale) * (CAP * LOG2E) + off)
            tot = tot + (weight[:, :128] + weight[:, 128:])
            wb[:, p * STEP : (p + 1) * STEP] = weight.astype(BF16)
        num = jnp.dot(wb[...], vb[...].reshape(2 * PH, BIAS), preferred_element_type=F32)
        part = 4 * ROWS
        po[k] = num[:part]
        for e in (2, 1, 3):
            pb[k, e - 1] = num[e * part : (e + 1) * part].astype(BF16)
            pl.when(c == 1)(give_back(k, e).start)
        row = lax.dot_general(
            jnp.ones((8, 128), BF16), tot.astype(BF16), (((1,), (1,)), ((), ())), preferred_element_type=F32
        )
        for e in range(NY):
            ty[e, k, :, :part] = row[:1, e * part : (e + 1) * part]

        @pl.when(k == 2)
        def _():
            for copy in totals_back[0]:
                copy.start()

        return carry

    lax.fori_loop(0, 4, attend, 0)
    sent += [give_back(k, e) for k in range(4) for e in (1, 2, 3)]

    for copy in totals_back[1]:
        copy.start()

    @pl.when(c == 1)
    def _():
        pl.semaphore_signal(turn, inc=1, device_id=sibling, device_id_type=MESH)

    @pl.when(c == 0)
    def _():
        pl.semaphore_wait(turn, 1)
        for k in range(4):
            for e in (2, 1, 3):
                give_back(k, e).start()

    sent += totals_back[0] + totals_back[1]

    add_up(0)
    add_up(1)
    add_up(2)
    add_totals(0)
    add_up(3)
    add_totals(1)
    sent += totals_out
    sent += [to_owner(k, j) for k in range(4) for j in (0, 1)]

    frames_out = [send(fr.at[0], fr.at[NX - e], s_xf.at[e - 1], r_xf.at[NX - e - 1], dev(dx=e)) for e in (2, 1, 3)]
    sent1 += frames_out

    @pl.when(c == 1)
    def _():
        for copy in frames_out:
            copy.start()

    for n in range(6, 10):
        loads[n].wait()

    half = D // 2
    context_out = [send(cx.at[0], cx.at[NX - e], s_xa.at[e - 1], r_xa.at[NX - e - 1], dev(dx=e)) for e in (2, 1, 3)]
    residual_over = send(rs.at[0, pl.ds(0, ROWS)], rc, s_rc, r_rc, sibling)
    parts_out = [
        [
            send(
                yo.at[h, e, pl.ds(core * ROWS, ROWS)],
                xr.at[h, (NX - e) % NX],
                s_xr.at[h, e * 2 + core],
                r_xr.at[h, (NX - e) % NX],
                dev(dx=e, core=core),
            )
            for e, core in ((2, 0), (2, 1), (1, 0), (1, 1), (3, 0), (3, 1), (0, 0))
        ]
        for h in (0, 1)
    ]
    sent1 += context_out + parts_out[0] + parts_out[1] + [residual_over]

    @pl.when(c == 1)
    def _():
        for e in (1, 3, 2):
            arrived(fr.at[e], r_xf.at[e - 1])
        total = jnp.zeros((2 * ROWS, BIAS), F32)
        for n in range(16):
            arrived(rz.at[n], r_rz.at[n])
            total = total + rz[n].astype(F32)
        arrived(tz, r_tz)
        even, odd = tz[0], tz[1]
        for n in range(2, 16, 2):
            even, odd = even + tz[n], odd + tz[n + 1]
        gap = lax.broadcasted_iota(jnp.int32, (2 * ROWS, 128), 1) - lax.broadcasted_iota(jnp.int32, (2 * ROWS, 128), 0)
        spread = jnp.where(gap == 0, even, 0.0) + jnp.where(gap == 2 * ROWS, odd, 0.0)
        context = total / jnp.sum(spread, axis=1, keepdims=True)
        power = jnp.mean(context * context, axis=1, keepdims=True)
        cx[0] = (context * lax.rsqrt(power + 0.0001)).astype(BF16)
        for copy in context_out:
            copy.start()
        for e in (1, 3, 2):
            arrived(cx.at[e], r_xa.at[e - 1])
        biased = jnp.dot(cx[...].reshape(NX * 2 * ROWS, BIAS), wo[...], preferred_element_type=F32)
        residual = (fr[...].reshape(NX * 2 * ROWS, D).astype(F32) + biased).astype(BF16)
        rs[...] = residual.reshape(NX, 2 * ROWS, D)
        residual_over.start()
        ffn_in = layer_norm(residual, ffg[...]).astype(BF16)
        hidden = gelu(jnp.dot(ffn_in, wu[...], preferred_element_type=F32)).astype(BF16)
        for h in (0, 1):
            part = jnp.dot(hidden, wd[:, h * half : (h + 1) * half], preferred_element_type=F32)
            yo[h] = part.astype(BF16).reshape(NX, 2 * ROWS, half)
            for copy in parts_out[h]:
                copy.start()
        for h in (0, 1):
            cols = slice(h * half, (h + 1) * half)
            done = rs[0, ROWS:, cols].astype(F32) + yo[h, 0, ROWS:, :].astype(F32)
            for e in (1, 3, 2):
                arrived(xr.at[h, e], r_xr.at[h, e])
                done = done + xr[h, e].astype(F32)
            out[:, cols] = done.astype(BF16)

    @pl.when(c == 0)
    def _():
        arrived(rc, r_rc)
        for h in (0, 1):
            cols = slice(h * half, (h + 1) * half)
            done = rc[:, cols].astype(F32)
            for e in (0, 1, 3, 2):
                arrived(xr.at[h, e], r_xr.at[h, e])
                done = done + xr[h, e].astype(F32)
            out[:, cols] = done.astype(BF16)

    finish()


def local(*args):
    dma = pltpu.SemaphoreType.DMA
    vm = pltpu.VMEM
    rows = 2 * ROWS
    return pl.pallas_call(
        kernel,
        out_shape=jax.ShapeDtypeStruct((ROWS, D), BF16),
        in_specs=[pl.BlockSpec(memory_space=pltpu.HBM)] * 10,
        out_specs=pl.BlockSpec(memory_space=pltpu.VMEM),
        scratch_shapes=[
            vm((NX, rows, D), BF16),
            vm((D,), F32),
            vm((D,), F32),
            vm((D, BIAS), BF16),
            vm((2, PH, BIAS), BF16),
            vm((2, PH, BIAS), BF16),
            vm((4, 256), jnp.int32),
            vm((BIAS, D), BF16),
            vm((D, FFL), BF16),
            vm((FFL, D), BF16),
            vm((rows, BIAS), BF16),
            vm((4, NY, 2 * rows, BIAS), BF16),
            vm((4, 3, 2 * rows, BIAS), BF16),
            vm((4, 2 * rows, BIAS), F32),
            vm((4, 3, 2 * rows, BIAS), BF16),
            vm((4, 2 * rows, BIAS), BF16),
            vm((16, rows, BIAS), BF16),
            vm((NY, 4, 1, 128), F32),
            vm((3, 4, 1, 128), F32),
            vm((4, 1, 128), F32),
            vm((16, 1, 128), F32),
            vm((NX, rows, BIAS), BF16),
            vm((NX, rows, D), BF16),
            vm((2, NX, rows, D // 2), BF16),
            vm((2, NX, ROWS, D // 2), BF16),
            vm((ROWS, D), BF16),
            vm((16, 128), F32),
            vm((STEP, 2 * PH), BF16),
            vm((rows, BIAS), BF16),
            dma((10,)),
            dma((2,)), dma((2,)),
            dma, dma,
            dma((10,)), dma((8,)), dma, dma((8,)),
            dma((4, 3)), dma((4, 3)),
            dma((4, 3)), dma((4, 3)),
            dma((8,)), dma((16,)),
            dma((2, 3)), dma((2, 3)),
            dma((8,)), dma,
            dma((3,)), dma((3,)),
            dma((3,)), dma((3,)),
            dma((2, 8)), dma((2, 4)),
            dma, dma,
            pltpu.SemaphoreType.REGULAR,
        ],
        compiler_params=pltpu.CompilerParams(
            collective_id=0, has_side_effects=True, vmem_limit_bytes=56 * 2**20
        ),
        name="layer",
    )(*args)


def solution(mesh):
    placed = (
        P(("dp", "bank"), None),
        P(),
        P(),
        P("bank", None),
        P("bank", None),
        P(),
        P(),
        P(),
        P(None, "dp"),
        P("dp", None),
    )
    return jax.shard_map(
        local, mesh=mesh, in_specs=placed, out_specs=P(("dp", "bank"), None), check_vma=False
    )
```

```python
import jax
import jax.numpy as jnp
from jax import lax
from jax.experimental import pallas as pl
from jax.experimental.pallas import tpu as pltpu
from jax.sharding import PartitionSpec as P

MESH = pl.DeviceIdType.MESH
F32 = jnp.float32
BF16 = jnp.bfloat16
CAP = 30.0
LOG2E = 1.4426950408889634
NEAR = (0, 1, -1, 2, -2, 3, -3, 4)
FAR = (-4, 5, -5, 6, -6, 7, -7, 8)
NZ, NY, NX = 16, 4, 4
D, FFL, BIAS = 1280, 640, 256
ROWS = 16
PH = 1024
STEP = 256


def layer_norm(values, gain):
    wide = values.astype(F32)
    center = jnp.mean(wide, axis=-1, keepdims=True)
    moved = wide - center
    spread = jnp.mean(moved * moved, axis=-1, keepdims=True)
    return moved * lax.rsqrt(spread + 1e-05) * gain[None, :]


def gelu(v):
    return 0.5 * v * (1.0 + lax.erf(v * 0.7071067811865476))


def kernel(
    frames, ln_gain, w_query, keys, values, active, w_out, ffn_gain, w_up, w_down, out,
    fr, lng, ffg, wq, kb, vb, act, wo, wu, wd,
    qown, qb, pb, po, ry, zs, rz, ty, tr, ts, tz, cx, rs, yo, xr, rc, bias, wb, upper,
    ld, s_kv, r_kv, s_fr, r_fr, s_q, r_q, r_up, s_fw, s_yf, r_yf, s_ry, r_ry, s_rz, r_rz,
    s_ty, r_ty, s_tz, r_tz, s_xf, r_xf, s_xa, r_xa, s_xr, r_xr, s_rc, r_rc, turn,
):
    x = lax.axis_index("dp")
    b = lax.axis_index("bank")
    c = lax.rem(b, 2)
    y = lax.rem(b // 2, NY)
    z = b // (2 * NY)

    def dev(dx=0, dz=0, dy=0, core=None):
        cz = lax.rem(z + dz + 2 * NZ, NZ)
        cy = lax.rem(y + dy + NY, NY)
        return (lax.rem(x + dx + NX, NX), (cz * NY + cy) * 2 + (c if core is None else core))

    sibling = dev(core=1 - c)

    def send(src, dst, ssem, rsem, to):
        return pltpu.make_async_remote_copy(
            src_ref=src, dst_ref=dst, send_sem=ssem, recv_sem=rsem, device_id=to, device_id_type=MESH
        )

    def arrived(dst, rsem):
        send(dst, dst, rsem, rsem, sibling).wait_recv()

    loads = [
        pltpu.make_async_copy(src, dst, ld.at[n])
        for n, (src, dst) in enumerate(
            (
                (frames, fr.at[0, pl.ds(ROWS, ROWS)]),
                (ln_gain, lng),
                (w_query, wq),
                (active, act),
                (keys, kb.at[c]),
                (values, vb.at[c]),
                (w_out, wo),
                (ffn_gain, ffg),
                (w_up, wu),
                (w_down, wd),
            )
        )
    ]
    for load in loads[:4]:
        load.start()

    sent, sent0, sent1 = [], [], []

    def finish():
        for copy in sent:
            copy.wait_send()

        @pl.when(c == 0)
        def _():
            for copy in sent0:
                copy.wait_send()

        @pl.when(c == 1)
        def _():
            for copy in sent1:
                copy.wait_send()

    barrier = pltpu.get_barrier_semaphore()

    def greet(to):
        pl.semaphore_signal(barrier, inc=1, device_id=to, device_id_type=MESH)

    @pl.when(c == 1)
    def _():
        greet(sibling)
        for dz in (4, -4, 3, -3, 2, -2, 1, -1):
            greet(dev(dz=dz))
        for e in (2, 1, 3):
            greet(dev(dy=e))
            greet(dev(dx=e))

    @pl.when(c == 0)
    def _():
        for dz in NEAR[::-1]:
            greet(dev(dz=dz, core=1))
        for e in (2, 1, 3):
            greet(dev(dy=e, core=1))
            greet(dev(dx=e, core=1))

    keys_over = send(keys, kb.at[c], s_kv.at[0], r_kv.at[0], sibling)
    values_over = send(values, vb.at[c], s_kv.at[1], r_kv.at[1], sibling)
    frames_over = send(frames, fr.at[0, pl.ds(0, ROWS)], s_fr, r_fr, sibling)

    def slot(i):
        return qb.at[i // 2, 0, pl.ds((i % 2) * 2 * ROWS, 2 * ROWS)]

    query_out = [
        send(qown, upper, s_q.at[9], r_up, dev(dz=-4, core=1)),
        send(qown, slot(0), s_q.at[8], r_q.at[0], dev(dz=4, core=1)),
    ] + [
        send(qown, slot(i), s_q.at[i], r_q.at[i], dev(dz=-NEAR[i], core=0)) for i in range(8)
    ]
    relay_down = [
        send(upper, slot(2 * n - 1), s_fw.at[2 * n - 1], r_q.at[2 * n - 1], dev(dz=-n, core=1)) for n in (4, 3, 2, 1)
    ]
    relay_up = [send(slot(0), slot(2 * n), s_fw.at[2 * n], r_q.at[2 * n], dev(dz=n, core=1)) for n in (3, 2, 1)]

    def forward(k, e):
        return send(qb.at[k, 0], qb.at[k, NY - e], s_yf.at[k, e - 1], r_yf.at[k, NY - e - 1], dev(dy=e))

    sent0 += [frames_over]
    sent1 += query_out + relay_down + relay_up
    sent += [keys_over, values_over]

    @pl.when(c == 0)
    def _():
        pl.semaphore_wait(barrier, 1)
        frames_over.start()
        for load in loads[4:]:
            load.start()
        for load in loads[:3]:
            load.wait()

    @pl.when(c == 1)
    def _():
        loads[0].wait()
        loads[1].wait()
        arrived(fr.at[0, pl.ds(0, ROWS)], r_fr)
        normed = layer_norm(fr[0], lng[...]).astype(BF16)
        loads[2].wait()
        qown[...] = jnp.dot(normed, wq[...], preferred_element_type=F32).astype(BF16)
        for load in loads[4:]:
            load.start()
        pl.semaphore_wait(barrier, 28)
        for copy in query_out:
            copy.start()

    keys_over.start()
    values_over.start()

    loads[3].wait()
    first = (z * NY + y) * 16
    ids = first + lax.broadcasted_iota(jnp.int32, (16, 256), 0)
    hits = jnp.where(ids == act[pl.ds(x, 1), :], 1.0, 0.0).astype(F32)
    found = jnp.max(hits, axis=1, keepdims=True)
    bias[...] = jnp.broadcast_to(jnp.where(found > 0.5, 0.0, -512.0).astype(F32), (16, 128))
    ty[...] = jnp.zeros_like(ty)

    @pl.when(c == 1)
    def _():
        arrived(upper, r_up)
        for copy in relay_down:
            copy.start()

    arrived(slot(0), r_q.at[0])

    @pl.when(c == 1)
    def _():
        for copy in relay_up:
            copy.start()

    for k in range(4):
        for i in (2 * k, 2 * k + 1):
            if i:
                arrived(slot(i), r_q.at[i])
        for e in (2, 1, 3):
            forward(k, e).start()
    sent += [forward(k, e) for k in range(4) for e in (1, 2, 3)]

    for n in range(4, 6):
        loads[n].wait()
    arrived(kb.at[1 - c], r_kv.at[0])
    arrived(vb.at[1 - c], r_kv.at[1])

    def give_back(k, e):
        return send(pb.at[k, e - 1], ry.at[k, NY - e - 1], s_ry.at[k, e - 1], r_ry.at[k, NY - e - 1], dev(dy=e))

    scale = 1.0 / (CAP * BIAS**0.5)

    def owner(i):
        return dev(dz=NEAR[i] + (FAR[i] - NEAR[i]) * c, core=1)

    def to_owner(k, j):
        i = 2 * k + j
        return send(
            zs.at[k, pl.ds(j * 2 * ROWS, 2 * ROWS)], rz.at[c * 8 + i], s_rz.at[i], r_rz.at[c * 8 + i], owner(i)
        )

    def add_up(k):
        total = po[k]
        for e in (1, 3, 2):
            arrived(ry.at[k, e - 1], r_ry.at[k, e - 1])
            total = total + ry[k, e - 1].astype(F32)
        zs[k] = total.astype(BF16)
        for j in (1, 0):
            to_owner(k, j).start()

    spans = (pl.ds(0, 3), pl.ds(3, 1))
    totals_back = [
        [
            send(ty.at[e, span], tr.at[NY - e - 1, span], s_ty.at[n, e - 1], r_ty.at[n, NY - e - 1], dev(dy=e))
            for e in (2, 1, 3)
        ]
        for n, span in enumerate(spans)
    ]
    totals_out = [
        send(ts.at[i // 2], tz.at[c * 8 + i], s_tz.at[i], r_tz, owner(i)) for i in range(8)
    ]

    def add_totals(n):
        span = spans[n]
        totals = ty[0, span]
        for e in (1, 3, 2):
            arrived(tr.at[e - 1, span], r_ty.at[n, e - 1])
            totals = totals + tr[e - 1, span]
        ts[span] = totals
        for copy in totals_out[6:] if n else totals_out[:6]:
            copy.start()

    def attend(k, carry):
        for e in (1, 3, 2):
            arrived(qb.at[k, e], r_yf.at[k, e - 1])
        q = qb[k].reshape(STEP, BIAS)
        tot = jnp.zeros((STEP, 128), F32)
        for p in range(2 * PH // STEP):
            h, at = (p * STEP) // PH, (p * STEP) % PH
            raw = lax.dot_general(
                q, kb[h, pl.ds(at, STEP), :], (((1,), (1,)), ((), ())), preferred_element_type=F32
            )
            off = jnp.concatenate([bias[pl.ds(2 * p, 1), :], bias[pl.ds(2 * p + 1, 1), :]], axis=1)
            weight = jnp.exp2(jnp.tanh(raw * scale) * (CAP * LOG2E) + off)
            tot = tot + (weight[:, :128] + weight[:, 128:])
            wb[:, p * STEP : (p + 1) * STEP] = weight.astype(BF16)
        num = jnp.dot(wb[...], vb[...].reshape(2 * PH, BIAS), preferred_element_type=F32)
        part = 4 * ROWS
        po[k] = num[:part]
        for e in (2, 1, 3):
            pb[k, e - 1] = num[e * part : (e + 1) * part].astype(BF16)
            pl.when(c == 1)(give_back(k, e).start)
        row = lax.dot_general(
            jnp.ones((8, 128), BF16), tot.astype(BF16), (((1,), (1,)), ((), ())), preferred_element_type=F32
        )
        for e in range(NY):
            ty[e, k, :, :part] = row[:1, e * part : (e + 1) * part]

        @pl.when(k == 2)
        def _():
            for copy in totals_back[0]:
                copy.start()

        return carry

    lax.fori_loop(0, 4, attend, 0)
    sent += [give_back(k, e) for k in range(4) for e in (1, 2, 3)]

    for copy in totals_back[1]:
        copy.start()

    @pl.when(c == 1)
    def _():
        pl.semaphore_signal(turn, inc=1, device_id=sibling, device_id_type=MESH)

    @pl.when(c == 0)
    def _():
        pl.semaphore_wait(turn, 1)
        for k in range(4):
            for e in (2, 1, 3):
                give_back(k, e).start()

    sent += totals_back[0] + totals_back[1]

    add_up(0)
    add_up(1)
    add_up(2)
    add_totals(0)
    add_up(3)
    add_totals(1)
    sent += totals_out
    sent += [to_owner(k, j) for k in range(4) for j in (0, 1)]

    frames_out = [send(fr.at[0], fr.at[NX - e], s_xf.at[e - 1], r_xf.at[NX - e - 1], dev(dx=e)) for e in (2, 1, 3)]
    sent1 += frames_out

    @pl.when(c == 1)
    def _():
        for copy in frames_out:
            copy.start()

    for n in range(6, 10):
        loads[n].wait()

    half = D // 2
    context_out = [send(cx.at[0], cx.at[NX - e], s_xa.at[e - 1], r_xa.at[NX - e - 1], dev(dx=e)) for e in (2, 1, 3)]
    residual_over = send(rs.at[0, pl.ds(0, ROWS)], rc, s_rc, r_rc, sibling)
    parts_out = [
        [
            send(
                yo.at[h, e, pl.ds(core * ROWS, ROWS)],
                xr.at[h, (NX - e) % NX],
                s_xr.at[h, e * 2 + core],
                r_xr.at[h, (NX - e) % NX],
                dev(dx=e, core=core),
            )
            for e, core in ((2, 0), (2, 1), (1, 0), (1, 1), (3, 0), (3, 1), (0, 0))
        ]
        for h in (0, 1)
    ]
    sent1 += context_out + parts_out[0] + parts_out[1] + [residual_over]

    @pl.when(c == 1)
    def _():
        for e in (1, 3, 2):
            arrived(fr.at[e], r_xf.at[e - 1])
        total = jnp.zeros((2 * ROWS, BIAS), F32)
        for n in range(16):
            arrived(rz.at[n], r_rz.at[n])
            total = total + rz[n].astype(F32)
        arrived(tz, r_tz)
        even, odd = tz[0], tz[1]
        for n in range(2, 16, 2):
            even, odd = even + tz[n], odd + tz[n + 1]
        gap = lax.broadcasted_iota(jnp.int32, (2 * ROWS, 128), 1) - lax.broadcasted_iota(jnp.int32, (2 * ROWS, 128), 0)
        spread = jnp.where(gap == 0, even, 0.0) + jnp.where(gap == 2 * ROWS, odd, 0.0)
        context = total / jnp.sum(spread, axis=1, keepdims=True)
        power = jnp.mean(context * context, axis=1, keepdims=True)
        cx[0] = (context * lax.rsqrt(power + 0.0001)).astype(BF16)
        for copy in context_out:
            copy.start()
        for e in (1, 3, 2):
            arrived(cx.at[e], r_xa.at[e - 1])
        biased = jnp.dot(cx[...].reshape(NX * 2 * ROWS, BIAS), wo[...], preferred_element_type=F32)
        residual = (fr[...].reshape(NX * 2 * ROWS, D).astype(F32) + biased).astype(BF16)
        rs[...] = residual.reshape(NX, 2 * ROWS, D)
        residual_over.start()
        ffn_in = layer_norm(residual, ffg[...]).astype(BF16)
        hidden = gelu(jnp.dot(ffn_in, wu[...], preferred_element_type=F32)).astype(BF16)
        for h in (0, 1):
            part = jnp.dot(hidden, wd[:, h * half : (h + 1) * half], preferred_element_type=F32)
            yo[h] = part.astype(BF16).reshape(NX, 2 * ROWS, half)
            for copy in parts_out[h]:
                copy.start()
        for h in (0, 1):
            cols = slice(h * half, (h + 1) * half)
            done = rs[0, ROWS:, cols].astype(F32) + yo[h, 0, ROWS:, :].astype(F32)
            for e in (1, 3, 2):
                arrived(xr.at[h, e], r_xr.at[h, e])
                done = done + xr[h, e].astype(F32)
            out[:, cols] = done.astype(BF16)

    @pl.when(c == 0)
    def _():
        arrived(rc, r_rc)
        for h in (0, 1):
            cols = slice(h * half, (h + 1) * half)
            done = rc[:, cols].astype(F32)
            for e in (0, 1, 3, 2):
                arrived(xr.at[h, e], r_xr.at[h, e])
                done = done + xr[h, e].astype(F32)
            out[:, cols] = done.astype(BF16)

    finish()


def local(*args):
    dma = pltpu.SemaphoreType.DMA
    vm = pltpu.VMEM
    rows = 2 * ROWS
    return pl.pallas_call(
        kernel,
        out_shape=jax.ShapeDtypeStruct((ROWS, D), BF16),
        in_specs=[pl.BlockSpec(memory_space=pltpu.HBM)] * 10,
        out_specs=pl.BlockSpec(memory_space=pltpu.VMEM),
        scratch_shapes=[
            vm((NX, rows, D), BF16),
            vm((D,), F32),
            vm((D,), F32),
            vm((D, BIAS), BF16),
            vm((2, PH, BIAS), BF16),
            vm((2, PH, BIAS), BF16),
            vm((4, 256), jnp.int32),
            vm((BIAS, D), BF16),
            vm((D, FFL), BF16),
            vm((FFL, D), BF16),
            vm((rows, BIAS), BF16),
            vm((4, NY, 2 * rows, BIAS), BF16),
            vm((4, 3, 2 * rows, BIAS), BF16),
            vm((4, 2 * rows, BIAS), F32),
            vm((4, 3, 2 * rows, BIAS), BF16),
            vm((4, 2 * rows, BIAS), BF16),
            vm((16, rows, BIAS), BF16),
            vm((NY, 4, 1, 128), F32),
            vm((3, 4, 1, 128), F32),
            vm((4, 1, 128), F32),
            vm((16, 1, 128), F32),
            vm((NX, rows, BIAS), BF16),
            vm((NX, rows, D), BF16),
            vm((2, NX, rows, D // 2), BF16),
            vm((2, NX, ROWS, D // 2), BF16),
            vm((ROWS, D), BF16),
            vm((16, 128), F32),
            vm((STEP, 2 * PH), BF16),
            vm((rows, BIAS), BF16),
            dma((10,)),
            dma((2,)), dma((2,)),
            dma, dma,
            dma((10,)), dma((8,)), dma, dma((8,)),
            dma((4, 3)), dma((4, 3)),
            dma((4, 3)), dma((4, 3)),
            dma((8,)), dma((16,)),
            dma((2, 3)), dma((2, 3)),
            dma((8,)), dma,
            dma((3,)), dma((3,)),
            dma((3,)), dma((3,)),
            dma((2, 8)), dma((2, 4)),
            dma, dma,
            pltpu.SemaphoreType.REGULAR,
        ],
        compiler_params=pltpu.CompilerParams(
            collective_id=0, has_side_effects=True, vmem_limit_bytes=56 * 2**20
        ),
        name="layer",
    )(*args)


def solution(mesh):
    placed = (
        P(("dp", "bank"), None),
        P(),
        P(),
        P("bank", None),
        P("bank", None),
        P(),
        P(),
        P(),
        P(None, "dp"),
        P("dp", None),
    )
    return jax.shard_map(
        local, mesh=mesh, in_specs=placed, out_specs=P(("dp", "bank"), None), check_vma=False
    )
```

```python
import jax
import jax.numpy as jnp
from jax import lax
from jax.experimental import pallas as pl
from jax.experimental.pallas import tpu as pltpu
from jax.sharding import PartitionSpec as P

MESH = pl.DeviceIdType.MESH
F32 = jnp.float32
BF16 = jnp.bfloat16
CAP = 30.0
LOG2E = 1.4426950408889634
NEAR = (0, 1, -1, 2, -2, 3, -3, 4)
FAR = (-4, 5, -5, 6, -6, 7, -7, 8)
NZ, NY, NX = 16, 4, 4
D, FFL, BIAS = 1280, 640, 256
ROWS = 16
PH = 1024
STEP = 256


def layer_norm(values, gain):
    wide = values.astype(F32)
    center = jnp.mean(wide, axis=-1, keepdims=True)
    moved = wide - center
    spread = jnp.mean(moved * moved, axis=-1, keepdims=True)
    return moved * lax.rsqrt(spread + 1e-05) * gain[None, :]


def gelu(v):
    return 0.5 * v * (1.0 + lax.erf(v * 0.7071067811865476))


def kernel(
    frames, ln_gain, w_query, keys, values, active, w_out, ffn_gain, w_up, w_down, out,
    fr, lng, ffg, wq, kb, vb, act, wo, wu, wd,
    qown, qb, pb, po, ry, zs, rz, ty, tr, ts, tz, cx, rs, yo, xr, rc, bias, wb, upper,
    ld, s_kv, r_kv, s_fr, r_fr, s_q, r_q, r_up, s_fw, s_yf, r_yf, s_ry, r_ry, s_rz, r_rz,
    s_ty, r_ty, s_tz, r_tz, s_xf, r_xf, s_xa, r_xa, s_xr, r_xr, s_rc, r_rc, turn,
):
    x = lax.axis_index("dp")
    b = lax.axis_index("bank")
    c = lax.rem(b, 2)
    y = lax.rem(b // 2, NY)
    z = b // (2 * NY)

    def dev(dx=0, dz=0, dy=0, core=None):
        cz = lax.rem(z + dz + 2 * NZ, NZ)
        cy = lax.rem(y + dy + NY, NY)
        return (lax.rem(x + dx + NX, NX), (cz * NY + cy) * 2 + (c if core is None else core))

    sibling = dev(core=1 - c)

    def send(src, dst, ssem, rsem, to):
        return pltpu.make_async_remote_copy(
            src_ref=src, dst_ref=dst, send_sem=ssem, recv_sem=rsem, device_id=to, device_id_type=MESH
        )

    def arrived(dst, rsem):
        send(dst, dst, rsem, rsem, sibling).wait_recv()

    loads = [
        pltpu.make_async_copy(src, dst, ld.at[n])
        for n, (src, dst) in enumerate(
            (
                (frames, fr.at[0, pl.ds(ROWS, ROWS)]),
                (ln_gain, lng),
                (w_query, wq),
                (active, act),
                (keys, kb.at[c]),
                (values, vb.at[c]),
                (w_out, wo),
                (ffn_gain, ffg),
                (w_up, wu),
                (w_down, wd),
            )
        )
    ]
    for load in loads[:4]:
        load.start()

    sent, sent0, sent1 = [], [], []

    def finish():
        for copy in sent:
            copy.wait_send()

        @pl.when(c == 0)
        def _():
            for copy in sent0:
                copy.wait_send()

        @pl.when(c == 1)
        def _():
            for copy in sent1:
                copy.wait_send()

    barrier = pltpu.get_barrier_semaphore()

    def greet(to):
        pl.semaphore_signal(barrier, inc=1, device_id=to, device_id_type=MESH)

    @pl.when(c == 1)
    def _():
        greet(sibling)
        for dz in (4, -4, 3, -3, 2, -2, 1, -1):
            greet(dev(dz=dz))
        for e in (2, 1, 3):
            greet(dev(dy=e))
            greet(dev(dx=e))

    @pl.when(c == 0)
    def _():
        for dz in NEAR[::-1]:
            greet(dev(dz=dz, core=1))
        for e in (2, 1, 3):
            greet(dev(dy=e, core=1))
            greet(dev(dx=e, core=1))

    keys_over = send(keys, kb.at[c], s_kv.at[0], r_kv.at[0], sibling)
    values_over = send(values, vb.at[c], s_kv.at[1], r_kv.at[1], sibling)
    frames_over = send(frames, fr.at[0, pl.ds(0, ROWS)], s_fr, r_fr, sibling)

    def slot(i):
        return qb.at[i // 2, 0, pl.ds((i % 2) * 2 * ROWS, 2 * ROWS)]

    query_out = [
        send(qown, upper, s_q.at[9], r_up, dev(dz=-4, core=1)),
        send(qown, slot(0), s_q.at[8], r_q.at[0], dev(dz=4, core=1)),
    ] + [
        send(qown, slot(i), s_q.at[i], r_q.at[i], dev(dz=-NEAR[i], core=0)) for i in range(8)
    ]
    relay_down = [
        send(upper, slot(2 * n - 1), s_fw.at[2 * n - 1], r_q.at[2 * n - 1], dev(dz=-n, core=1)) for n in (1, 2, 3, 4)
    ]
    relay_up = [send(slot(0), slot(2 * n), s_fw.at[2 * n], r_q.at[2 * n], dev(dz=n, core=1)) for n in (1, 2, 3)]

    def forward(k, e):
        return send(qb.at[k, 0], qb.at[k, NY - e], s_yf.at[k, e - 1], r_yf.at[k, NY - e - 1], dev(dy=e))

    sent0 += [frames_over]
    sent1 += query_out + relay_down + relay_up
    sent += [keys_over, values_over]

    @pl.when(c == 0)
    def _():
        pl.semaphore_wait(barrier, 1)
        frames_over.start()
        for load in loads[4:]:
            load.start()
        for load in loads[:3]:
            load.wait()

    @pl.when(c == 1)
    def _():
        loads[0].wait()
        loads[1].wait()
        arrived(fr.at[0, pl.ds(0, ROWS)], r_fr)
        normed = layer_norm(fr[0], lng[...]).astype(BF16)
        loads[2].wait()
        qown[...] = jnp.dot(normed, wq[...], preferred_element_type=F32).astype(BF16)
        for load in loads[4:]:
            load.start()
        pl.semaphore_wait(barrier, 28)
        for copy in query_out:
            copy.start()

    keys_over.start()
    values_over.start()

    loads[3].wait()
    first = (z * NY + y) * 16
    ids = first + lax.broadcasted_iota(jnp.int32, (16, 256), 0)
    hits = jnp.where(ids == act[pl.ds(x, 1), :], 1.0, 0.0).astype(F32)
    found = jnp.max(hits, axis=1, keepdims=True)
    bias[...] = jnp.broadcast_to(jnp.where(found > 0.5, 0.0, -512.0).astype(F32), (16, 128))
    ty[...] = jnp.zeros_like(ty)

    @pl.when(c == 1)
    def _():
        arrived(upper, r_up)
        for copy in relay_down:
            copy.start()

    arrived(slot(0), r_q.at[0])

    @pl.when(c == 1)
    def _():
        for copy in relay_up:
            copy.start()

    for k in range(4):
        for i in (2 * k, 2 * k + 1):
            if i:
                arrived(slot(i), r_q.at[i])
        for e in (2, 1, 3):
            forward(k, e).start()
    sent += [forward(k, e) for k in range(4) for e in (1, 2, 3)]

    for n in range(4, 6):
        loads[n].wait()
    arrived(kb.at[1 - c], r_kv.at[0])
    arrived(vb.at[1 - c], r_kv.at[1])

    def give_back(k, e):
        return send(pb.at[k, e - 1], ry.at[k, NY - e - 1], s_ry.at[k, e - 1], r_ry.at[k, NY - e - 1], dev(dy=e))

    scale = 1.0 / (CAP * BIAS**0.5)

    def owner(i):
        return dev(dz=NEAR[i] + (FAR[i] - NEAR[i]) * c, core=1)

    def to_owner(k, j):
        i = 2 * k + j
        return send(
            zs.at[k, pl.ds(j * 2 * ROWS, 2 * ROWS)], rz.at[c * 8 + i], s_rz.at[i], r_rz.at[c * 8 + i], owner(i)
        )

    def add_up(k):
        total = po[k]
        for e in (1, 3, 2):
            arrived(ry.at[k, e - 1], r_ry.at[k, e - 1])
            total = total + ry[k, e - 1].astype(F32)
        zs[k] = total.astype(BF16)
        for j in (1, 0):
            to_owner(k, j).start()

    spans = (pl.ds(0, 3), pl.ds(3, 1))
    totals_back = [
        [
            send(ty.at[e, span], tr.at[NY - e - 1, span], s_ty.at[n, e - 1], r_ty.at[n, NY - e - 1], dev(dy=e))
            for e in (2, 1, 3)
        ]
        for n, span in enumerate(spans)
    ]
    totals_out = [
        send(ts.at[i // 2], tz.at[c * 8 + i], s_tz.at[i], r_tz, owner(i)) for i in range(8)
    ]

    def add_totals(n):
        span = spans[n]
        totals = ty[0, span]
        for e in (1, 3, 2):
            arrived(tr.at[e - 1, span], r_ty.at[n, e - 1])
            totals = totals + tr[e - 1, span]
        ts[span] = totals
        for copy in totals_out[6:] if n else totals_out[:6]:
            copy.start()

    def attend(k, carry):
        for e in (1, 3, 2):
            arrived(qb.at[k, e], r_yf.at[k, e - 1])
        q = qb[k].reshape(STEP, BIAS)
        tot = jnp.zeros((STEP, 128), F32)
        for p in range(2 * PH // STEP):
            h, at = (p * STEP) // PH, (p * STEP) % PH
            raw = lax.dot_general(
                q, kb[h, pl.ds(at, STEP), :], (((1,), (1,)), ((), ())), preferred_element_type=F32
            )
            off = jnp.concatenate([bias[pl.ds(2 * p, 1), :], bias[pl.ds(2 * p + 1, 1), :]], axis=1)
            weight = jnp.exp2(jnp.tanh(raw * scale) * (CAP * LOG2E) + off)
            tot = tot + (weight[:, :128] + weight[:, 128:])
            wb[:, p * STEP : (p + 1) * STEP] = weight.astype(BF16)
        num = jnp.dot(wb[...], vb[...].reshape(2 * PH, BIAS), preferred_element_type=F32)
        part = 4 * ROWS
        po[k] = num[:part]
        for e in (2, 1, 3):
            pb[k, e - 1] = num[e * part : (e + 1) * part].astype(BF16)
            pl.when(c == 1)(give_back(k, e).start)
        row = lax.dot_general(
            jnp.ones((8, 128), BF16), tot.astype(BF16), (((1,), (1,)), ((), ())), preferred_element_type=F32
        )
        for e in range(NY):
            ty[e, k, :, :part] = row[:1, e * part : (e + 1) * part]

        @pl.when(k == 2)
        def _():
            for copy in totals_back[0]:
                copy.start()

        return carry

    lax.fori_loop(0, 4, attend, 0)
    sent += [give_back(k, e) for k in range(4) for e in (1, 2, 3)]

    for copy in totals_back[1]:
        copy.start()

    @pl.when(c == 1)
    def _():
        pl.semaphore_signal(turn, inc=1, device_id=sibling, device_id_type=MESH)

    @pl.when(c == 0)
    def _():
        pl.semaphore_wait(turn, 1)
        for k in range(4):
            for e in (2, 1, 3):
                give_back(k, e).start()

    sent += totals_back[0] + totals_back[1]

    add_up(0)
    add_up(1)
    add_up(2)
    add_totals(0)
    add_up(3)
    add_totals(1)
    sent += totals_out
    sent += [to_owner(k, j) for k in range(4) for j in (0, 1)]

    frames_out = [send(fr.at[0], fr.at[NX - e], s_xf.at[e - 1], r_xf.at[NX - e - 1], dev(dx=e)) for e in (2, 1, 3)]
    sent1 += frames_out

    @pl.when(c == 1)
    def _():
        for copy in frames_out:
            copy.start()

    for n in range(6, 10):
        loads[n].wait()

    half = D // 2
    context_out = [send(cx.at[0], cx.at[NX - e], s_xa.at[e - 1], r_xa.at[NX - e - 1], dev(dx=e)) for e in (2, 1, 3)]
    residual_over = send(rs.at[0, pl.ds(0, ROWS)], rc, s_rc, r_rc, sibling)
    parts_out = [
        [
            send(
                yo.at[h, e, pl.ds(core * ROWS, ROWS)],
                xr.at[h, (NX - e) % NX],
                s_xr.at[h, e * 2 + core],
                r_xr.at[h, (NX - e) % NX],
                dev(dx=e, core=core),
            )
            for e, core in ((2, 0), (2, 1), (1, 0), (1, 1), (3, 0), (3, 1), (0, 0))
        ]
        for h in (0, 1)
    ]
    sent1 += context_out + parts_out[0] + parts_out[1] + [residual_over]

    @pl.when(c == 1)
    def _():
        for e in (1, 3, 2):
            arrived(fr.at[e], r_xf.at[e - 1])
        total = jnp.zeros((2 * ROWS, BIAS), F32)
        for n in range(16):
            arrived(rz.at[n], r_rz.at[n])
            total = total + rz[n].astype(F32)
        arrived(tz, r_tz)
        even, odd = tz[0], tz[1]
        for n in range(2, 16, 2):
            even, odd = even + tz[n], odd + tz[n + 1]
        gap = lax.broadcasted_iota(jnp.int32, (2 * ROWS, 128), 1) - lax.broadcasted_iota(jnp.int32, (2 * ROWS, 128), 0)
        spread = jnp.where(gap == 0, even, 0.0) + jnp.where(gap == 2 * ROWS, odd, 0.0)
        context = total / jnp.sum(spread, axis=1, keepdims=True)
        power = jnp.mean(context * context, axis=1, keepdims=True)
        cx[0] = (context * lax.rsqrt(power + 0.0001)).astype(BF16)
        for copy in context_out:
            copy.start()
        for e in (1, 3, 2):
            arrived(cx.at[e], r_xa.at[e - 1])
        biased = jnp.dot(cx[...].reshape(NX * 2 * ROWS, BIAS), wo[...], preferred_element_type=F32)
        residual = (fr[...].reshape(NX * 2 * ROWS, D).astype(F32) + biased).astype(BF16)
        rs[...] = residual.reshape(NX, 2 * ROWS, D)
        residual_over.start()
        ffn_in = layer_norm(residual, ffg[...]).astype(BF16)
        hidden = gelu(jnp.dot(ffn_in, wu[...], preferred_element_type=F32)).astype(BF16)
        for h in (0, 1):
            part = jnp.dot(hidden, wd[:, h * half : (h + 1) * half], preferred_element_type=F32)
            yo[h] = part.astype(BF16).reshape(NX, 2 * ROWS, half)
            for copy in parts_out[h]:
                copy.start()
        for h in (0, 1):
            cols = slice(h * half, (h + 1) * half)
            done = rs[0, ROWS:, cols].astype(F32) + yo[h, 0, ROWS:, :].astype(F32)
            for e in (1, 3, 2):
                arrived(xr.at[h, e], r_xr.at[h, e])
                done = done + xr[h, e].astype(F32)
            out[:, cols] = done.astype(BF16)

    @pl.when(c == 0)
    def _():
        arrived(rc, r_rc)
        for h in (0, 1):
            cols = slice(h * half, (h + 1) * half)
            done = rc[:, cols].astype(F32)
            for e in (0, 1, 3, 2):
                arrived(xr.at[h, e], r_xr.at[h, e])
                done = done + xr[h, e].astype(F32)
            out[:, cols] = done.astype(BF16)

    finish()


def local(*args):
    dma = pltpu.SemaphoreType.DMA
    vm = pltpu.VMEM
    rows = 2 * ROWS
    return pl.pallas_call(
        kernel,
        out_shape=jax.ShapeDtypeStruct((ROWS, D), BF16),
        in_specs=[pl.BlockSpec(memory_space=pltpu.HBM)] * 10,
        out_specs=pl.BlockSpec(memory_space=pltpu.VMEM),
        scratch_shapes=[
            vm((NX, rows, D), BF16),
            vm((D,), F32),
            vm((D,), F32),
            vm((D, BIAS), BF16),
            vm((2, PH, BIAS), BF16),
            vm((2, PH, BIAS), BF16),
            vm((4, 256), jnp.int32),
            vm((BIAS, D), BF16),
            vm((D, FFL), BF16),
            vm((FFL, D), BF16),
            vm((rows, BIAS), BF16),
            vm((4, NY, 2 * rows, BIAS), BF16),
            vm((4, 3, 2 * rows, BIAS), BF16),
            vm((4, 2 * rows, BIAS), F32),
            vm((4, 3, 2 * rows, BIAS), BF16),
            vm((4, 2 * rows, BIAS), BF16),
            vm((16, rows, BIAS), BF16),
            vm((NY, 4, 1, 128), F32),
            vm((3, 4, 1, 128), F32),
            vm((4, 1, 128), F32),
            vm((16, 1, 128), F32),
            vm((NX, rows, BIAS), BF16),
            vm((NX, rows, D), BF16),
            vm((2, NX, rows, D // 2), BF16),
            vm((2, NX, ROWS, D // 2), BF16),
            vm((ROWS, D), BF16),
            vm((16, 128), F32),
            vm((STEP, 2 * PH), BF16),
            vm((rows, BIAS), BF16),
            dma((10,)),
            dma((2,)), dma((2,)),
            dma, dma,
            dma((10,)), dma((8,)), dma, dma((8,)),
            dma((4, 3)), dma((4, 3)),
            dma((4, 3)), dma((4, 3)),
            dma((8,)), dma((16,)),
            dma((2, 3)), dma((2, 3)),
            dma((8,)), dma,
            dma((3,)), dma((3,)),
            dma((3,)), dma((3,)),
            dma((2, 8)), dma((2, 4)),
            dma, dma,
            pltpu.SemaphoreType.REGULAR,
        ],
        compiler_params=pltpu.CompilerParams(
            collective_id=0, has_side_effects=True, vmem_limit_bytes=56 * 2**20
        ),
        name="layer",
    )(*args)


def solution(mesh):
    placed = (
        P(("dp", "bank"), None),
        P(),
        P(),
        P("bank", None),
        P("bank", None),
        P(),
        P(),
        P(),
        P(None, "dp"),
        P("dp", None),
    )
    return jax.shard_map(
        local, mesh=mesh, in_specs=placed, out_specs=P(("dp", "bank"), None), check_vma=False
    )
```

```python
import jax
import jax.numpy as jnp
from jax import lax
from jax.experimental import pallas as pl
from jax.experimental.pallas import tpu as pltpu
from jax.sharding import PartitionSpec as P

MESH = pl.DeviceIdType.MESH
F32 = jnp.float32
BF16 = jnp.bfloat16
CAP = 30.0
LOG2E = 1.4426950408889634
NEAR = (0, 1, -1, 2, -2, 3, -3, 4)
FAR = (-4, 5, -5, 6, -6, 7, -7, 8)
NZ, NY, NX = 16, 4, 4
D, FFL, BIAS = 1280, 640, 256
ROWS = 16
PH = 1024
STEP = 256


def layer_norm(values, gain):
    wide = values.astype(F32)
    center = jnp.mean(wide, axis=-1, keepdims=True)
    moved = wide - center
    spread = jnp.mean(moved * moved, axis=-1, keepdims=True)
    return moved * lax.rsqrt(spread + 1e-05) * gain[None, :]


def gelu(v):
    return 0.5 * v * (1.0 + lax.erf(v * 0.7071067811865476))


def kernel(
    frames, ln_gain, w_query, keys, values, active, w_out, ffn_gain, w_up, w_down, out,
    fr, lng, ffg, wq, kb, vb, act, wo, wu, wd,
    qown, qb, pb, po, ry, zs, rz, ty, tr, ts, tz, cx, rs, yo, xr, rc, bias, wb, upper,
    ld, s_kv, r_kv, s_fr, r_fr, s_q, r_q, r_up, s_fw, s_yf, r_yf, s_ry, r_ry, s_rz, r_rz,
    s_ty, r_ty, s_tz, r_tz, s_xf, r_xf, s_xa, r_xa, s_xr, r_xr, s_rc, r_rc, turn,
):
    x = lax.axis_index("dp")
    b = lax.axis_index("bank")
    c = lax.rem(b, 2)
    y = lax.rem(b // 2, NY)
    z = b // (2 * NY)

    def dev(dx=0, dz=0, dy=0, core=None):
        cz = lax.rem(z + dz + 2 * NZ, NZ)
        cy = lax.rem(y + dy + NY, NY)
        return (lax.rem(x + dx + NX, NX), (cz * NY + cy) * 2 + (c if core is None else core))

    sibling = dev(core=1 - c)

    def send(src, dst, ssem, rsem, to):
        return pltpu.make_async_remote_copy(
            src_ref=src, dst_ref=dst, send_sem=ssem, recv_sem=rsem, device_id=to, device_id_type=MESH
        )

    def arrived(dst, rsem):
        send(dst, dst, rsem, rsem, sibling).wait_recv()

    loads = [
        pltpu.make_async_copy(src, dst, ld.at[n])
        for n, (src, dst) in enumerate(
            (
                (frames, fr.at[0, pl.ds(ROWS, ROWS)]),
                (ln_gain, lng),
                (w_query, wq),
                (active, act),
                (keys, kb.at[c]),
                (values, vb.at[c]),
                (w_out, wo),
                (ffn_gain, ffg),
                (w_up, wu),
                (w_down, wd),
            )
        )
    ]
    for load in loads[:4]:
        load.start()

    sent, sent0, sent1 = [], [], []

    def finish():
        for copy in sent:
            copy.wait_send()

        @pl.when(c == 0)
        def _():
            for copy in sent0:
                copy.wait_send()

        @pl.when(c == 1)
        def _():
            for copy in sent1:
                copy.wait_send()

    barrier = pltpu.get_barrier_semaphore()

    def greet(to):
        pl.semaphore_signal(barrier, inc=1, device_id=to, device_id_type=MESH)

    @pl.when(c == 1)
    def _():
        greet(sibling)
        for dz in (4, -4, 3, -3, 2, -2, 1, -1):
            greet(dev(dz=dz))
        for e in (2, 1, 3):
            greet(dev(dy=e))
            greet(dev(dx=e))

    @pl.when(c == 0)
    def _():
        for dz in NEAR[::-1]:
            greet(dev(dz=dz, core=1))
        for e in (2, 1, 3):
            greet(dev(dy=e, core=1))
            greet(dev(dx=e, core=1))

    keys_over = send(keys, kb.at[c], s_kv.at[0], r_kv.at[0], sibling)
    values_over = send(values, vb.at[c], s_kv.at[1], r_kv.at[1], sibling)
    frames_over = send(frames, fr.at[0, pl.ds(0, ROWS)], s_fr, r_fr, sibling)

    def slot(i):
        return qb.at[i // 2, 0, pl.ds((i % 2) * 2 * ROWS, 2 * ROWS)]

    query_out = [
        send(qown, upper, s_q.at[9], r_up, dev(dz=-4, core=1)),
        send(qown, slot(0), s_q.at[8], r_q.at[0], dev(dz=4, core=1)),
    ] + [
        send(qown, slot(i), s_q.at[i], r_q.at[i], dev(dz=-NEAR[i], core=0)) for i in range(8)
    ]
    relay_down = [
        send(upper, slot(2 * n - 1), s_fw.at[2 * n - 1], r_q.at[2 * n - 1], dev(dz=-n, core=1)) for n in (1, 2, 3, 4)
    ]
    relay_up = [send(slot(0), slot(2 * n), s_fw.at[2 * n], r_q.at[2 * n], dev(dz=n, core=1)) for n in (1, 2, 3)]

    def forward(k, e):
        return send(qb.at[k, 0], qb.at[k, NY - e], s_yf.at[k, e - 1], r_yf.at[k, NY - e - 1], dev(dy=e))

    sent0 += [frames_over]
    sent1 += query_out + relay_down + relay_up
    sent += [keys_over, values_over]

    @pl.when(c == 0)
    def _():
        pl.semaphore_wait(barrier, 1)
        frames_over.start()
        for load in loads[4:]:
            load.start()
        for load in loads[:3]:
            load.wait()

    @pl.when(c == 1)
    def _():
        loads[0].wait()
        loads[1].wait()
        arrived(fr.at[0, pl.ds(0, ROWS)], r_fr)
        normed = layer_norm(fr[0], lng[...]).astype(BF16)
        loads[2].wait()
        qown[...] = jnp.dot(normed, wq[...], preferred_element_type=F32).astype(BF16)
        for load in loads[4:]:
            load.start()
        pl.semaphore_wait(barrier, 28)
        for copy in query_out:
            copy.start()

    @pl.when(c == 0)
    def _():
        keys_over.start()
        values_over.start()

    loads[3].wait()
    first = (z * NY + y) * 16
    ids = first + lax.broadcasted_iota(jnp.int32, (16, 256), 0)
    hits = jnp.where(ids == act[pl.ds(x, 1), :], 1.0, 0.0).astype(F32)
    found = jnp.max(hits, axis=1, keepdims=True)
    bias[...] = jnp.broadcast_to(jnp.where(found > 0.5, 0.0, -512.0).astype(F32), (16, 128))
    ty[...] = jnp.zeros_like(ty)

    @pl.when(c == 1)
    def _():
        arrived(upper, r_up)
        for copy in relay_down:
            copy.start()

    arrived(slot(0), r_q.at[0])

    @pl.when(c == 1)
    def _():
        for copy in relay_up:
            copy.start()
        keys_over.start()
        values_over.start()

    for k in range(4):
        for i in (2 * k, 2 * k + 1):
            if i:
                arrived(slot(i), r_q.at[i])
        for e in (2, 1, 3):
            forward(k, e).start()
    sent += [forward(k, e) for k in range(4) for e in (1, 2, 3)]

    for n in range(4, 6):
        loads[n].wait()
    arrived(kb.at[1 - c], r_kv.at[0])
    arrived(vb.at[1 - c], r_kv.at[1])

    def give_back(k, e):
        return send(pb.at[k, e - 1], ry.at[k, NY - e - 1], s_ry.at[k, e - 1], r_ry.at[k, NY - e - 1], dev(dy=e))

    scale = 1.0 / (CAP * BIAS**0.5)

    def owner(i):
        return dev(dz=NEAR[i] + (FAR[i] - NEAR[i]) * c, core=1)

    def to_owner(k, j):
        i = 2 * k + j
        return send(
            zs.at[k, pl.ds(j * 2 * ROWS, 2 * ROWS)], rz.at[c * 8 + i], s_rz.at[i], r_rz.at[c * 8 + i], owner(i)
        )

    def add_up(k):
        total = po[k]
        for e in (1, 3, 2):
            arrived(ry.at[k, e - 1], r_ry.at[k, e - 1])
            total = total + ry[k, e - 1].astype(F32)
        zs[k] = total.astype(BF16)
        for j in (1, 0):
            to_owner(k, j).start()

    spans = (pl.ds(0, 3), pl.ds(3, 1))
    totals_back = [
        [
            send(ty.at[e, span], tr.at[NY - e - 1, span], s_ty.at[n, e - 1], r_ty.at[n, NY - e - 1], dev(dy=e))
            for e in (2, 1, 3)
        ]
        for n, span in enumerate(spans)
    ]
    totals_out = [
        send(ts.at[i // 2], tz.at[c * 8 + i], s_tz.at[i], r_tz, owner(i)) for i in range(8)
    ]

    def add_totals(n):
        span = spans[n]
        totals = ty[0, span]
        for e in (1, 3, 2):
            arrived(tr.at[e - 1, span], r_ty.at[n, e - 1])
            totals = totals + tr[e - 1, span]
        ts[span] = totals
        for copy in totals_out[6:] if n else totals_out[:6]:
            copy.start()

    def attend(k, carry):
        for e in (1, 3, 2):
            arrived(qb.at[k, e], r_yf.at[k, e - 1])
        q = qb[k].reshape(STEP, BIAS)
        tot = jnp.zeros((STEP, 128), F32)
        for p in range(2 * PH // STEP):
            h, at = (p * STEP) // PH, (p * STEP) % PH
            raw = lax.dot_general(
                q, kb[h, pl.ds(at, STEP), :], (((1,), (1,)), ((), ())), preferred_element_type=F32
            )
            off = jnp.concatenate([bias[pl.ds(2 * p, 1), :], bias[pl.ds(2 * p + 1, 1), :]], axis=1)
            weight = jnp.exp2(jnp.tanh(raw * scale) * (CAP * LOG2E) + off)
            tot = tot + (weight[:, :128] + weight[:, 128:])
            wb[:, p * STEP : (p + 1) * STEP] = weight.astype(BF16)
        num = jnp.dot(wb[...], vb[...].reshape(2 * PH, BIAS), preferred_element_type=F32)
        part = 4 * ROWS
        po[k] = num[:part]
        for e in (2, 1, 3):
            pb[k, e - 1] = num[e * part : (e + 1) * part].astype(BF16)
            pl.when(c == 1)(give_back(k, e).start)
        row = lax.dot_general(
            jnp.ones((8, 128), BF16), tot.astype(BF16), (((1,), (1,)), ((), ())), preferred_element_type=F32
        )
        for e in range(NY):
            ty[e, k, :, :part] = row[:1, e * part : (e + 1) * part]

        @pl.when(k == 2)
        def _():
            for copy in totals_back[0]:
                copy.start()

        return carry

    lax.fori_loop(0, 4, attend, 0)
    sent += [give_back(k, e) for k in range(4) for e in (1, 2, 3)]

    for copy in totals_back[1]:
        copy.start()

    @pl.when(c == 1)
    def _():
        pl.semaphore_signal(turn, inc=1, device_id=sibling, device_id_type=MESH)

    @pl.when(c == 0)
    def _():
        pl.semaphore_wait(turn, 1)
        for k in range(4):
            for e in (2, 1, 3):
                give_back(k, e).start()

    sent += totals_back[0] + totals_back[1]

    add_up(0)
    add_up(1)
    add_up(2)
    add_totals(0)
    add_up(3)
    add_totals(1)
    sent += totals_out
    sent += [to_owner(k, j) for k in range(4) for j in (0, 1)]

    frames_out = [send(fr.at[0], fr.at[NX - e], s_xf.at[e - 1], r_xf.at[NX - e - 1], dev(dx=e)) for e in (2, 1, 3)]
    sent1 += frames_out

    @pl.when(c == 1)
    def _():
        for copy in frames_out:
            copy.start()

    for n in range(6, 10):
        loads[n].wait()

    half = D // 2
    context_out = [send(cx.at[0], cx.at[NX - e], s_xa.at[e - 1], r_xa.at[NX - e - 1], dev(dx=e)) for e in (2, 1, 3)]
    residual_over = send(rs.at[0, pl.ds(0, ROWS)], rc, s_rc, r_rc, sibling)
    parts_out = [
        [
            send(
                yo.at[h, e, pl.ds(core * ROWS, ROWS)],
                xr.at[h, (NX - e) % NX],
                s_xr.at[h, e * 2 + core],
                r_xr.at[h, (NX - e) % NX],
                dev(dx=e, core=core),
            )
            for e, core in ((2, 0), (2, 1), (1, 0), (1, 1), (3, 0), (3, 1), (0, 0))
        ]
        for h in (0, 1)
    ]
    sent1 += context_out + parts_out[0] + parts_out[1] + [residual_over]

    @pl.when(c == 1)
    def _():
        for e in (1, 3, 2):
            arrived(fr.at[e], r_xf.at[e - 1])
        total = jnp.zeros((2 * ROWS, BIAS), F32)
        for n in range(16):
            arrived(rz.at[n], r_rz.at[n])
            total = total + rz[n].astype(F32)
        arrived(tz, r_tz)
        even, odd = tz[0], tz[1]
        for n in range(2, 16, 2):
            even, odd = even + tz[n], odd + tz[n + 1]
        gap = lax.broadcasted_iota(jnp.int32, (2 * ROWS, 128), 1) - lax.broadcasted_iota(jnp.int32, (2 * ROWS, 128), 0)
        spread = jnp.where(gap == 0, even, 0.0) + jnp.where(gap == 2 * ROWS, odd, 0.0)
        context = total / jnp.sum(spread, axis=1, keepdims=True)
        power = jnp.mean(context * context, axis=1, keepdims=True)
        cx[0] = (context * lax.rsqrt(power + 0.0001)).astype(BF16)
        for copy in context_out:
            copy.start()
        for e in (1, 3, 2):
            arrived(cx.at[e], r_xa.at[e - 1])
        biased = jnp.dot(cx[...].reshape(NX * 2 * ROWS, BIAS), wo[...], preferred_element_type=F32)
        residual = (fr[...].reshape(NX * 2 * ROWS, D).astype(F32) + biased).astype(BF16)
        rs[...] = residual.reshape(NX, 2 * ROWS, D)
        residual_over.start()
        ffn_in = layer_norm(residual, ffg[...]).astype(BF16)
        hidden = gelu(jnp.dot(ffn_in, wu[...], preferred_element_type=F32)).astype(BF16)
        for h in (0, 1):
            part = jnp.dot(hidden, wd[:, h * half : (h + 1) * half], preferred_element_type=F32)
            yo[h] = part.astype(BF16).reshape(NX, 2 * ROWS, half)
            for copy in parts_out[h]:
                copy.start()
        for h in (0, 1):
            cols = slice(h * half, (h + 1) * half)
            done = rs[0, ROWS:, cols].astype(F32) + yo[h, 0, ROWS:, :].astype(F32)
            for e in (1, 3, 2):
                arrived(xr.at[h, e], r_xr.at[h, e])
                done = done + xr[h, e].astype(F32)
            out[:, cols] = done.astype(BF16)

    @pl.when(c == 0)
    def _():
        arrived(rc, r_rc)
        for h in (0, 1):
            cols = slice(h * half, (h + 1) * half)
            done = rc[:, cols].astype(F32)
            for e in (0, 1, 3, 2):
                arrived(xr.at[h, e], r_xr.at[h, e])
                done = done + xr[h, e].astype(F32)
            out[:, cols] = done.astype(BF16)

    finish()


def local(*args):
    dma = pltpu.SemaphoreType.DMA
    vm = pltpu.VMEM
    rows = 2 * ROWS
    return pl.pallas_call(
        kernel,
        out_shape=jax.ShapeDtypeStruct((ROWS, D), BF16),
        in_specs=[pl.BlockSpec(memory_space=pltpu.HBM)] * 10,
        out_specs=pl.BlockSpec(memory_space=pltpu.VMEM),
        scratch_shapes=[
            vm((NX, rows, D), BF16),
            vm((D,), F32),
            vm((D,), F32),
            vm((D, BIAS), BF16),
            vm((2, PH, BIAS), BF16),
            vm((2, PH, BIAS), BF16),
            vm((4, 256), jnp.int32),
            vm((BIAS, D), BF16),
            vm((D, FFL), BF16),
            vm((FFL, D), BF16),
            vm((rows, BIAS), BF16),
            vm((4, NY, 2 * rows, BIAS), BF16),
            vm((4, 3, 2 * rows, BIAS), BF16),
            vm((4, 2 * rows, BIAS), F32),
            vm((4, 3, 2 * rows, BIAS), BF16),
            vm((4, 2 * rows, BIAS), BF16),
            vm((16, rows, BIAS), BF16),
            vm((NY, 4, 1, 128), F32),
            vm((3, 4, 1, 128), F32),
            vm((4, 1, 128), F32),
            vm((16, 1, 128), F32),
            vm((NX, rows, BIAS), BF16),
            vm((NX, rows, D), BF16),
            vm((2, NX, rows, D // 2), BF16),
            vm((2, NX, ROWS, D // 2), BF16),
            vm((ROWS, D), BF16),
            vm((16, 128), F32),
            vm((STEP, 2 * PH), BF16),
            vm((rows, BIAS), BF16),
            dma((10,)),
            dma((2,)), dma((2,)),
            dma, dma,
            dma((10,)), dma((8,)), dma, dma((8,)),
            dma((4, 3)), dma((4, 3)),
            dma((4, 3)), dma((4, 3)),
            dma((8,)), dma((16,)),
            dma((2, 3)), dma((2, 3)),
            dma((8,)), dma,
            dma((3,)), dma((3,)),
            dma((3,)), dma((3,)),
            dma((2, 8)), dma((2, 4)),
            dma, dma,
            pltpu.SemaphoreType.REGULAR,
        ],
        compiler_params=pltpu.CompilerParams(
            collective_id=0, has_side_effects=True, vmem_limit_bytes=56 * 2**20
        ),
        name="layer",
    )(*args)


def solution(mesh):
    placed = (
        P(("dp", "bank"), None),
        P(),
        P(),
        P("bank", None),
        P("bank", None),
        P(),
        P(),
        P(),
        P(None, "dp"),
        P("dp", None),
    )
    return jax.shard_map(
        local, mesh=mesh, in_specs=placed, out_specs=P(("dp", "bank"), None), check_vma=False
    )
```
